128 devices in a mesh: box: 8 (over z, y_lo), dir: 16 (over y_hi, x, core).
Axes of the slice: x: 4, y: 4 (y_hi: 2, y_lo: 2; y = y_hi * 2 + y_lo), z: 4, core: 2. Of those that a mesh axis runs over, the one named last changes fastest.
Arguments:
- child_rad: float32 [800, 16, 2, 2, 384], P('dir', 'box'), may hold values from -6 to 6
- box_at_slot: int32 [8], replicated, may hold values from 0 to 7, each once
- octant: int32 [16], replicated, may hold values from 0 to 7, as said below
- far_par: int32 [8, 3], replicated, may hold values from 0 to 7, as said below
- far_par_off: int32 [8, 3], replicated, may hold values from 0 to 7
- far_child: int32 [16, 7], replicated, may hold values from 0 to 15, as said below
- far_child_off: int32 [16, 7], replicated, may hold values from 0 to 15
- far_child_count: int32 [16], replicated, may hold values from 2 to 7
- trans_par: float32 [1600, 8, 2, 768], P('dir'), may hold values from -1.8 to 1.8
- trans_child: float32 [800, 16, 2, 384], P('dir'), may hold values from -1.8 to 1.8
Outputs:
- child_in: float32 [800, 16, 2, 2, 384], P('dir', 'box')
The draws below stay inside these ranges and needn't reach their ends.
Inputs may be any that keep to these rules, and one draw needn't show every extreme that they name: `box_at_slot`: a permutation of the parent boxes. `octant`: the children of one parent box lie in different octants. `far_par`: row b lists 3 different parent boxes, none of them b. `far_child`: row c lists 7 different child boxes, none of them c; only the first far_child_count[c] entries are used.
All inputs are finite; a program needn't handle non-finite values.
Results may differ from the reference program's by a relative error of at most 0.00018.
Values sent between devices are 32-bit elements; how exact they have to be, the bound alone decides.
A program may use at most 128 MiB of HBM per device.

```python
import math
import jax
import jax.numpy as jnp
from jax import lax

NT_C = 384
NP_C = 800
KIDS = 2
FAR_P = 3
FAR_C = 7
OFF_P = 8
OFF_C = 16
NT_P = 768
NP_P = 1600
NB_P = 8
NB_C = 16


def distinct_others(row_key, count, chosen):
    row_keys = jax.random.split(row_key, count)

    def shuffle_row(single_key):
        return jax.random.permutation(single_key, count - 1)
    orders = jax.vmap(shuffle_row)(row_keys).astype(jnp.int32)
    row_index = jnp.arange(count, dtype=jnp.int32)[:, None]
    return ((row_index + 1 + orders[:, :chosen]) % count).astype(jnp.int32)


def place_value(table, row_pick, kid_pick, wanted):
    row_index = jnp.arange(NB_P, dtype=jnp.int32)[:, None]
    kid_index = jnp.arange(KIDS, dtype=jnp.int32)[None, :]
    present = jnp.any(table[row_pick] == wanted)
    target = (row_index == row_pick) & (kid_index == kid_pick) & jnp.logical_not(present)
    return jnp.where(target, wanted, table).astype(jnp.int32)


def draw_octant(key, part):
    key = jax.random.fold_in(key, 11)
    perm_key, row_key, kid_key, low_key = jax.random.split(key, 4)
    row_keys = jax.random.split(perm_key, NB_P)

    def pick_octants(single_key):
        return jax.random.permutation(single_key, 8)[:KIDS]
    table = jax.vmap(pick_octants)(row_keys).astype(jnp.int32)
    top_row = jax.random.randint(row_key, (), 0, NB_P).astype(jnp.int32)
    top_kid = jax.random.randint(kid_key, (), 0, KIDS).astype(jnp.int32)
    low_row = ((top_row + 1) % NB_P).astype(jnp.int32)
    low_kid = jax.random.randint(low_key, (), 0, KIDS).astype(jnp.int32)
    table = place_value(table, top_row, top_kid, 7)
    table = place_value(table, low_row, low_kid, 0)
    return table.reshape(-1).astype(jnp.int32)


def draw_far_par(key, part):
    key = jax.random.fold_in(key, 12)
    return distinct_others(key, NB_P, FAR_P)


def draw_far_child(key, part):
    key = jax.random.fold_in(key, 13)
    return distinct_others(key, NB_C, FAR_C)


def draw_far_child_count(key, part):
    key = jax.random.fold_in(key, 14)
    sparse_key, start_key = jax.random.split(key)
    sparse_len = jax.random.randint(sparse_key, (NB_C,), 2, FAR_C // 2 + 1)
    dense_start = jax.random.randint(start_key, (), 0, NB_C - 3)
    box_index = jnp.arange(NB_C, dtype=jnp.int32)
    dense_mask = (box_index >= dense_start) & (box_index < dense_start + 4)
    return jnp.where(dense_mask, FAR_C, sparse_len).astype(jnp.int32)


def with_ends(drawn, stream_key, low, top_value):
    spot = [jax.random.randint(jax.random.fold_in(stream_key, axis), (), 0, length) for axis, length in enumerate(drawn.shape)]
    longest = drawn.shape.index(max(drawn.shape))
    next_to = spot[:longest] + [(spot[longest] + 1) % drawn.shape[longest]] + spot[longest + 1:]
    return drawn.at[tuple(spot)].set(low).at[tuple(next_to)].set(top_value)


def block_scale(own_key, shape, pieces, low, top_value):
    loudness, own = 1.0, jax.random.fold_in(own_key, 6)
    for axis_at, parts in pieces:
        heights = jnp.exp(jax.random.uniform(jax.random.fold_in(own, axis_at), (parts,), jnp.float32, low / len(pieces), top_value / len(pieces)))
        loudness = loudness * jnp.repeat(heights, shape[axis_at] // parts).reshape([-1 if axis == axis_at else 1 for axis in range(len(shape))])
    return loudness


def noise(own_key, dims, scale, bound, cuts=(), kind=jnp.bfloat16):
    values = jax.random.normal(own_key, dims, jnp.float32) * scale
    if len(cuts) > 0:
        values = block_scale(own_key, dims, cuts, -0.22, 0.18) * values
    return jnp.clip(values, min=-bound, max=bound).astype(kind)


def setup_inputs(seed: int = 0) -> dict:
    splits = jax.random.split(jax.random.key(seed), 11)
    child_rad = noise(splits[0], (NP_C, NB_C, 2, 2, NT_C), 1.0, 6.0, ((0, 16), (1, 8)), jnp.float32)
    box_at_slot = jax.random.permutation(splits[1], NB_P).astype(jnp.int32)
    octant = draw_octant(jax.random.fold_in(splits[10], 71), 0)
    far_par = draw_far_par(jax.random.fold_in(splits[10], 71), 0)
    far_par_off = with_ends(jax.random.randint(splits[4], (NB_P, FAR_P), 0, OFF_P), jax.random.fold_in(splits[4], 1), 0, OFF_P - 1).astype(jnp.int32)
    far_child = draw_far_child(jax.random.fold_in(splits[10], 71), 0)
    far_child_off = with_ends(jax.random.randint(splits[6], (NB_C, FAR_C), 0, OFF_C), jax.random.fold_in(splits[6], 1), 0, OFF_C - 1).astype(jnp.int32)
    far_child_count = draw_far_child_count(jax.random.fold_in(splits[10], 71), 0)
    trans_par = noise(splits[8], (NP_P, OFF_P, 2, NT_P), 0.3, 1.8, ((0, 16),), jnp.float32)
    trans_child = noise(splits[9], (NP_C, OFF_C, 2, NT_C), 0.3, 1.8, ((0, 16),), jnp.float32)
    return dict(child_rad=child_rad, box_at_slot=box_at_slot, octant=octant, far_par=far_par, far_par_off=far_par_off, far_child=far_child, far_child_off=far_child_off, far_child_count=far_child_count, trans_par=trans_par, trans_child=trans_child)


offset_phase = 32.0 * math.pi
highest = lax.Precision.HIGHEST


def theta_table(child_count):
    parent_rows = jnp.arange(2 * child_count, dtype=jnp.int32)
    lowest = (parent_rows - 1) // 2
    first_node = jnp.clip(lowest - 2, 0, child_count - 6)
    offset = parent_rows.astype(jnp.float32) * 0.5 - 0.25 - first_node.astype(jnp.float32)
    columns = jnp.arange(child_count, dtype=jnp.int32)
    lagrange = jnp.zeros((2 * child_count, child_count), jnp.float32)
    for node_index in range(6):
        weight = jnp.ones_like(offset)
        for other_node in range(6):
            if other_node != node_index:
                weight = weight * (offset - float(other_node)) / float(node_index - other_node)
        match_mask = (columns[None, :] == (first_node + node_index)[:, None]).astype(jnp.float32)
        lagrange = lagrange + weight[:, None] * match_mask
    return lagrange


def phi_kernel(parent_index, child_index, child_count):
    period = 4 * child_count
    parity_odd = 2 * parent_index - 4 * child_index - 1
    numerator = jnp.mod((child_count - 1) * parity_odd, 2 * period).astype(jnp.float32)
    denominator = parity_odd.astype(jnp.float32)
    return jnp.sin(math.pi * numerator / period) / (child_count * jnp.sin(math.pi * denominator / period))


def directions(phi_index, phi_count, theta_count):
    theta_angle = (jnp.arange(theta_count, dtype=jnp.int32).astype(jnp.float32) + 0.5) * (math.pi / theta_count)
    phi_angle = (phi_index.astype(jnp.float32) + 0.5) * (2.0 * math.pi / phi_count)
    sin_theta = jnp.sin(theta_angle)[None, :]
    east_part = sin_theta * jnp.cos(phi_angle)[:, None]
    north_part = sin_theta * jnp.sin(phi_angle)[:, None]
    upward = jnp.broadcast_to(jnp.cos(theta_angle)[None, :], east_part.shape)
    return east_part, north_part, upward


def rotate(pattern, octants, east_part, north_part, upward, phase_sign):
    sign_east = (jnp.mod(octants, 2) * 2 - 1).astype(jnp.float32)
    sign_north = (jnp.mod(octants // 2, 2) * 2 - 1).astype(jnp.float32)
    sign_up = (jnp.mod(octants // 4, 2) * 2 - 1).astype(jnp.float32)
    angle_all = offset_phase * (sign_east[None, :, None] * east_part[:, None, :]
                                + sign_north[None, :, None] * north_part[:, None, :]
                                + sign_up[None, :, None] * upward[:, None, :])
    cosine = jnp.cos(angle_all)[:, :, None, :]
    sine_part = phase_sign * jnp.sin(angle_all)[:, :, None, :]
    real_part = pattern[:, :, 0]
    imag_part = pattern[:, :, 1]
    return jnp.stack([cosine * real_part - sine_part * imag_part, sine_part * real_part + cosine * imag_part], axis=2)


def complex_mul(translation, pattern):
    table_real = translation[:, :, 0][:, :, None, :]
    table_imag = translation[:, :, 1][:, :, None, :]
    field_real = pattern[:, :, 0]
    field_imag = pattern[:, :, 1]
    return jnp.stack([table_real * field_real - table_imag * field_imag,
                      table_real * field_imag + table_imag * field_real], axis=2)


def reference(child_rad, box_at_slot, octant, far_par, far_par_off, far_child, far_child_off, far_child_count, trans_par, trans_child):
    theta_map = theta_table(NT_C)
    phi_map = phi_kernel(jnp.arange(NP_P, dtype=jnp.int32)[:, None], jnp.arange(NP_C, dtype=jnp.int32)[None, :], NP_C)
    east_part, north_part, upward = directions(jnp.arange(NP_P, dtype=jnp.int32), NP_P, NT_P)
    slot_lookup = jnp.argsort(box_at_slot).astype(jnp.int32)
    kid_boxes = (box_at_slot[:, None] * KIDS + jnp.arange(KIDS, dtype=jnp.int32)[None, :]).reshape(-1)
    kid_octants = jnp.take(octant, kid_boxes)
    spread = jnp.einsum("pc,cnabt->pnabt", phi_map, child_rad, precision=highest)
    widened = jnp.einsum("pnabt,qt->pnabq", spread, theta_map, precision=highest)
    shifted = rotate(widened, kid_octants, east_part, north_part, upward, 1.0)
    parent_rad = shifted.reshape(NP_P, NB_P, KIDS, 2, 2, NT_P).sum(axis=2)
    parent_in = jnp.zeros_like(parent_rad)
    for far_slot in range(FAR_P):
        source_slot = jnp.take(slot_lookup, jnp.take(far_par[:, far_slot], box_at_slot))
        picked = jnp.take(parent_rad, source_slot, axis=1)
        tables = jnp.take(trans_par, jnp.take(far_par_off[:, far_slot], box_at_slot), axis=1)
        parent_in = parent_in + complex_mul(tables, picked)
    returned = rotate(jnp.repeat(parent_in, KIDS, axis=1), kid_octants, east_part, north_part, upward, -1.0)
    narrowed = 0.5 * jnp.einsum("pnabq,qt->pnabt", returned, theta_map, precision=highest)
    descended = 0.5 * jnp.einsum("pc,pnabt->cnabt", phi_map, narrowed, precision=highest)
    counts = jnp.take(far_child_count, kid_boxes)
    child_far = jnp.zeros_like(child_rad)
    for far_slot in range(FAR_C):
        source_ids = jnp.take(far_child[:, far_slot], kid_boxes)
        source_slot = jnp.take(slot_lookup, source_ids // KIDS) * KIDS + source_ids % KIDS
        picked = jnp.take(child_rad, source_slot, axis=1)
        tables = jnp.take(trans_child, jnp.take(far_child_off[:, far_slot], kid_boxes), axis=1)
        active = (far_slot < counts)[None, :, None, None, None]
        child_far = child_far + jnp.where(active, complex_mul(tables, picked), 0.0)
    return descended + child_far
```

```python
import functools
import math

import jax
import jax.numpy as jnp
import numpy as np
from jax import lax
from jax.experimental import pallas as pl
from jax.experimental.pallas import tpu as pltpu
from jax.sharding import PartitionSpec as P

T_CHILD, P_CHILD = 384, 800
T_PARENT, P_PARENT = 768, 1600
FAR_P, FAR_C = 3, 7

PARTS = 3
LANES = 128
GROUP = 7
MESH = pl.DeviceIdType.MESH
F32, BF16 = jnp.float32, jnp.bfloat16


def split_np(table):
    high = table.astype(np.float32).astype(jnp.bfloat16)
    low = (table - high.astype(np.float64)).astype(np.float32).astype(jnp.bfloat16)
    return high, low


@functools.cache
def theta_tables():
    q = np.arange(T_PARENT)
    first = np.clip((q - 1) // 2 - 2, 0, T_CHILD - 6)
    offset = q * 0.5 - 0.25 - first
    table = np.zeros((T_PARENT, T_CHILD))
    for node in range(6):
        weight = np.ones(T_PARENT)
        for other in range(6):
            if other != node:
                weight = weight * (offset - other) / (node - other)
        table[q, first + node] = weight
    part, pair, place, i = np.meshgrid(np.arange(PARTS), np.arange(32), np.arange(2), np.arange(4), indexing="ij")
    wide, narrow = [], []
    for kid in range(2):
        chip = 2 * pair + (place if kid == 0 else 1 - place)
        rows = table[(12 * chip + 4 * part + i).reshape(-1)]
        wide.append(np.stack(split_np(rows)))
        back = 0.25 * rows.reshape(PARTS, 256, T_CHILD).transpose(0, 2, 1)
        narrow.append(np.stack(split_np(back)))
    return np.stack(wide), np.stack(narrow)


@functools.cache
def phi_tables():
    p = np.arange(P_PARENT)[:, None]
    c = np.arange(P_CHILD)[None, :]
    odd = 2 * p - 4 * c - 1
    period = 4 * P_CHILD
    numerator = np.mod((P_CHILD - 1) * odd, 2 * period).astype(np.float64)
    table = np.sin(math.pi * numerator / period) / (P_CHILD * np.sin(math.pi * odd / period))
    plus = np.zeros((4 * LANES, 8 * LANES))
    minus = np.zeros((4 * LANES, 8 * LANES))
    f = np.arange(50)
    row_of = 8 * (f // GROUP) + f % GROUP
    for jj in range(4):
        for core in range(2):
            child = 100 * jj + 50 * core + f
            rows = jj * LANES + core * 64 + row_of
            for dd in range(8):
                parent = 100 * dd + np.arange(100)
                near = table[np.ix_(parent, child)].T
                far = table[np.ix_(parent, child + 400)].T
                at = np.ix_(rows, dd * LANES + np.arange(100))
                plus[at] = 0.5 * (near + far)
                minus[at] = 0.5 * (near - far)
    return np.stack([np.stack(split_np(plus)), np.stack(split_np(minus))])


@functools.cache
def phi_angles():
    lane = np.arange(16 * LANES)
    phi = 2.0 * math.pi * (100 * (lane // LANES) + lane % LANES + 0.5) / P_PARENT
    return np.stack([np.cos(phi), np.sin(phi)]).reshape(2, 1, 16 * LANES).astype(np.float32)


def split(x):
    high = x.astype(BF16)
    return high, (x - high.astype(F32)).astype(BF16)


NT = (((1,), (1,)), ((), ()))
NN = (((1,), (0,)), ((), ()))


def mul(a, b, dims):
    return lax.dot_general(a, b, dims, preferred_element_type=F32)


def kernel(
    bas, octant, far_par, far_par_off, far_child, far_child_off, far_count,
    x_in, tab_in, tabc, wide, narrow, weights, angles,
    out,
    slot_of, oct_lo, oct_hi, par_src, par_off, kid_src, kid_kid, kid_off, kid_act,
    x_swap, x_hi, x_lo, send1, recv1, send2, recv2,
    child_recv, far_out, far_recv, tab_recv, tab, etab, y, pr, r_hi, r_lo, acc, own, res_recv,
    s_swap, s_child, s_far, s_tab, s_tabf, s_main, s_back, s_loc,
):
    b = lax.axis_index("box")
    d = lax.axis_index("dir")
    core = lax.rem(d, 2)
    j = d // 2
    me = b * 8 + j
    chip_odd = lax.rem(j, 2) == 1
    buddy = (b, d + 1 - 2 * core)

    def chip(t):
        return (t // 8, lax.rem(t, 8) * 2 + core)

    barrier = pltpu.get_barrier_semaphore()
    pl.semaphore_signal(barrier, inc=1, device_id=buddy, device_id_type=MESH)

    def greet(i, carry):
        pl.semaphore_signal(barrier, inc=1, device_id=chip(lax.rem(me + i, 64)), device_id_type=MESH)
        return carry

    lax.fori_loop(1, 64, greet, 0)

    for box in range(8):
        place = jnp.int32(0)
        for s in range(8):
            place = jnp.where(bas[s] == box, s, place)
        slot_of[box] = place
    for s in range(8):
        box = bas[s]
        o0, o1 = octant[2 * box], octant[2 * box + 1]
        oct_lo[s] = jnp.where(chip_odd, o1, o0)
        oct_hi[s] = jnp.where(chip_odd, o0, o1)
        for k in range(FAR_P):
            par_src[s * FAR_P + k] = slot_of[far_par[box, k]]
            par_off[s * FAR_P + k] = far_par_off[box, k]

    def kid_entry(n, carry):
        box = bas[n // 2] * 2 + lax.rem(n, 2)
        for k in range(FAR_C):
            source = far_child[box, k]
            kid_src[n * FAR_C + k] = slot_of[source // 2]
            kid_kid[n * FAR_C + k] = lax.rem(source, 2)
            kid_off[n * FAR_C + k] = far_child_off[box, k]
            kid_act[n * FAR_C + k] = jnp.where(k < far_count[box], 1.0, 0.0).astype(F32)
        return carry

    lax.fori_loop(0, 16, kid_entry, 0)

    def own_half(c, carry):
        for k in range(2):
            high, low = split(x_in[core, c, k])
            at = pl.ds(pl.multiple_of(core * 64, 64), 64)
            x_hi[c, k, at, :] = high
            x_lo[c, k, at, :] = low
        return carry

    lax.fori_loop(0, 2, own_half, 0)

    pl.semaphore_wait(barrier, 64)

    swap = pltpu.make_async_remote_copy(
        src_ref=x_in.at[1 - core], dst_ref=x_swap, send_sem=s_swap.at[0], recv_sem=s_swap.at[1],
        device_id=buddy, device_id_type=MESH)
    swap.start()

    def child_copy(g):
        return pltpu.make_async_remote_copy(
            src_ref=x_in.at[:, :, :, pl.ds(pl.multiple_of(g * 8, 8), 8), :], dst_ref=child_recv.at[b],
            send_sem=s_child.at[0], recv_sem=s_child.at[1], device_id=(g, d), device_id_type=MESH)

    def child_start(i, carry):
        child_copy(lax.rem(b + i, 8)).start()
        return carry

    lax.fori_loop(1, 8, child_start, 0)
    child_own = pltpu.make_async_copy(
        x_in.at[:, :, :, pl.ds(pl.multiple_of(b * 8, 8), 8), :], child_recv.at[b], s_loc.at[0])
    child_own.start()

    def tab_start(i, carry):
        to = lax.rem(j + i, 8)
        pltpu.make_async_remote_copy(
            src_ref=tab_in.at[to], dst_ref=tab_recv.at[core, j], send_sem=s_tab.at[0], recv_sem=s_tab.at[1],
            device_id=(b, to * 2 + core), device_id_type=MESH).start()
        return carry

    lax.fori_loop(1, 8, tab_start, 0)
    tab_own = pltpu.make_async_copy(tab_in.at[j], tab_recv.at[core, j], s_loc.at[1])
    tab_own.start()

    swap.wait()

    def other_half(c, carry):
        for k in range(2):
            high, low = split(x_swap[c, k])
            at = pl.ds(pl.multiple_of(64 - core * 64, 64), 64)
            x_hi[c, k, at, :] = high
            x_lo[c, k, at, :] = low
        return carry

    lax.fori_loop(0, 2, other_half, 0)

    lower = lax.broadcasted_iota(jnp.int32, (8, LANES), 0) < 4

    def main_copy(part, t, send, recv, sems):
        return pltpu.make_async_remote_copy(
            src_ref=send.at[part, t], dst_ref=recv.at[part, me],
            send_sem=sems.at[0, part], recv_sem=sems.at[1, part], device_id=chip(t), device_id_type=MESH)

    def send_all(part, send, recv, sems):
        def start(i, carry):
            main_copy(part, lax.rem(me + i, 64), send, recv, sems).start()
            return carry

        lax.fori_loop(1, 64, start, 0)
        recv[part, me] = send[part, me]

    def wait_all(part, ref, sem):
        span = ref.at[part, pl.ds(0, 63)]
        pltpu.make_async_copy(span, span, sem).wait()

    def widen(part, carry):
        rows = pl.ds(pl.multiple_of(part * 256, 256), 256)
        for c in range(2):
            got = []
            for k in range(2):
                hi, lo = x_hi[c, k], x_lo[c, k]
                th, tl = wide[k, 0, rows, :], wide[k, 1, rows, :]
                got.append(mul(th, hi, NT) + mul(th, lo, NT) + mul(tl, hi, NT))
            k0 = got[0].reshape(32, 8, LANES)
            k1 = got[1].reshape(32, 8, LANES)
            m = lower[None]
            even = jnp.where(m, k0, k1)
            odd = jnp.where(m, k1, k0)
            both = jnp.stack([even, odd], axis=1).reshape(64, 8, LANES)
            send1[part, :, c * 8:c * 8 + 8, :] = both
        send_all(part, send1, recv1, s_main)
        return carry

    lax.fori_loop(0, PARTS, widen, 0)

    tab_own.wait()
    span = tab_recv.at[core, pl.ds(0, 7)]
    pltpu.make_async_copy(span, span, s_tab.at[1]).wait()
    tab_on = pltpu.make_async_remote_copy(
        src_ref=tab_recv.at[core], dst_ref=tab_recv.at[core], send_sem=s_tabf.at[0], recv_sem=s_tabf.at[1],
        device_id=buddy, device_id_type=MESH)
    tab_on.start()

    child_own.wait()
    span = child_recv.at[pl.ds(0, 7)]
    pltpu.make_async_copy(span, span, s_child.at[1]).wait()

    def far_slot(s, carry):
        for kid in range(2):
            n = s * 2 + kid
            total = [[jnp.zeros((8, T_CHILD), F32) for _ in range(2)] for _ in range(2)]
            for k in range(FAR_C):
                src, sk, off = kid_src[n * FAR_C + k], kid_kid[n * FAR_C + k], kid_off[n * FAR_C + k]
                act = kid_act[n * FAR_C + k]
                tr, ti = tabc[off, 0] * act, tabc[off, 1] * act
                for p in range(2):
                    xr, xi = child_recv[src, p, 0, sk], child_recv[src, p, 1, sk]
                    total[p][0] = total[p][0] + (tr * xr - ti * xi)
                    total[p][1] = total[p][1] + (tr * xi + ti * xr)
            for p in range(2):
                for c in range(2):
                    far_out[s, p, c, kid] = total[p][c]
        return carry

    lax.fori_loop(0, 8, far_slot, 0)

    def far_start(i, carry):
        to = lax.rem(b + i, 8)
        pltpu.make_async_remote_copy(
            src_ref=far_out.at[to], dst_ref=far_recv.at[b], send_sem=s_far.at[0], recv_sem=s_far.at[1],
            device_id=(to, d), device_id_type=MESH).start()
        return carry

    lax.fori_loop(1, 8, far_start, 0)
    far_recv[b] = far_out[b]

    tab_on.wait()

    row = lax.broadcasted_iota(jnp.int32, (8, LANES), 0)

    def one_part(part, carry):
        q = (12 * me + 4 * part + lax.rem(row, 4)).astype(F32)
        theta = (q + 0.5) * (math.pi / T_PARENT)
        st, ct = 16.0 * jnp.sin(theta), 16.0 * jnp.cos(theta)

        def prepare(blk, carry):
            at = pl.ds(pl.multiple_of(blk * LANES, LANES), LANES)
            ux, uy = st * angles[0, :, at], st * angles[1, :, at]
            for o in range(4):
                t = ct + (ux if o % 2 else -ux) + (uy if o // 2 else -uy)
                f = t - jnp.round(t)
                a = f * f
                s = f * (3.14159265358979 + a * (-5.16771278004997 + a * (2.55016403987735 + a * (
                    -0.599264529320792 + a * (0.0821458866111282 + a * (-0.00737043094571435
                    + a * 0.000466302805767613))))))
                c = 1.0 + a * (-4.93480220054468 + a * (4.05871212641677 + a * (-1.33526276885459 + a * (
                    0.235330630358893 + a * (-0.0258068913900141 + a * (0.00192957430940392
                    - a * 0.000104638104924846))))))
                cos, sin = 1.0 - 2.0 * (s * s), 2.0 * (s * c)
                etab[4 + o, 0, :, at] = cos
                etab[4 + o, 1, :, at] = sin
                etab[3 - o, 0, :, at] = cos
                etab[3 - o, 1, :, at] = -sin
            dcore, dj = lax.rem(blk, 2), blk // 2
            for off in range(8):
                v = tab_recv[dcore, dj, part, off]
                w = pltpu.roll(v, 4, 0)
                tab[off, 0, :, at] = jnp.where(lower, v, w)
                tab[off, 1, :, at] = jnp.where(lower, w, v)
            return carry

        lax.fori_loop(0, 16, prepare, 0)

        wait_all(part, recv1, s_main.at[1, part])

        got = recv1[part].reshape(8, 8, 16, LANES)
        for sign in range(2):
            pieces = []
            for jj in range(4):
                one, two = got[:, jj], got[:, jj + 4]
                pieces.append((one + two if sign == 0 else one - two).reshape(128, LANES))
            high, low = split(jnp.concatenate(pieces, axis=1))
            for n in range(4):
                cols = slice(n * 256, n * 256 + 256)
                wh, wl = weights[sign, 0, :, cols], weights[sign, 1, :, cols]
                y[sign, :, cols] = mul(high, wh, NN) + mul(low, wh, NN) + mul(high, wl, NN)

        def block(dd, carry):
            for half in range(2):
                at_y = pl.ds(pl.multiple_of(dd * LANES, LANES), LANES)
                at = pl.ds(pl.multiple_of((dd + 8 * half) * LANES, LANES), LANES)
                for s in range(8):
                    yp = y[0, s * 16:s * 16 + 16, at_y]
                    ym = y[1, s * 16:s * 16 + 16, at_y]
                    v = yp + ym if half == 0 else yp - ym
                    vr, vi = v[:8], v[8:]
                    cos = jnp.where(lower, etab[oct_lo[s], 0, :, at], etab[oct_hi[s], 0, :, at])
                    sin = jnp.where(lower, etab[oct_lo[s], 1, :, at], etab[oct_hi[s], 1, :, at])
                    re = cos * vr - sin * vi
                    im = sin * vr + cos * vi
                    pr[half, s, 0] = re + pltpu.roll(re, 4, 0)
                    pr[half, s, 1] = im + pltpu.roll(im, 4, 0)
            for s in range(8):
                back = []
                for half in range(2):
                    at = pl.ds(pl.multiple_of((dd + 8 * half) * LANES, LANES), LANES)
                    re = im = None
                    for k in range(FAR_P):
                        src, off = par_src[s * FAR_P + k], par_off[s * FAR_P + k]
                        fr, fi = pr[half, src, 0], pr[half, src, 1]
                        tr, ti = tab[off, 0, :, at], tab[off, 1, :, at]
                        gr, gi = tr * fr - ti * fi, tr * fi + ti * fr
                        re = gr if re is None else re + gr
                        im = gi if im is None else im + gi
                    cos = jnp.where(lower, etab[oct_lo[s], 0, :, at], etab[oct_hi[s], 0, :, at])
                    sin = jnp.where(lower, etab[oct_lo[s], 1, :, at], etab[oct_hi[s], 1, :, at])
                    back.append(jnp.concatenate([cos * re + sin * im, cos * im - sin * re], axis=0))
                at_y = pl.ds(pl.multiple_of(dd * LANES, LANES), LANES)
                for sign in range(2):
                    high, low = split(back[0] + back[1] if sign == 0 else back[0] - back[1])
                    r_hi[sign, s * 16:s * 16 + 16, at_y] = high
                    r_lo[sign, s * 16:s * 16 + 16, at_y] = low
            return carry

        lax.fori_loop(0, 8, block, 0)

        z = []
        for sign in range(2):
            high, low = r_hi[sign], r_lo[sign]
            wh, wl = weights[sign, 0], weights[sign, 1]
            z.append(mul(high, wh, NT) + mul(low, wh, NT) + mul(high, wl, NT))
        one, two = z[0] + z[1], z[0] - z[1]
        for jj in range(4):
            cols = slice(jj * LANES, jj * LANES + LANES)
            a = one[:, cols].reshape(8, 16, LANES)
            c = two[:, cols].reshape(8, 16, LANES)
            for s in range(8):
                send2[part, s * 8 + jj] = a[s]
                send2[part, s * 8 + jj + 4] = c[s]
        send_all(part, send2, recv2, s_back)
        return carry

    lax.fori_loop(0, PARTS, one_part, 0)

    def narrow_part(part, carry):
        wait_all(part, recv2, s_back.at[1, part])
        got = recv2[part].reshape(32, 2, 16, LANES)
        for c in range(2):
            even = got[:, 0, c * 8:c * 8 + 8]
            odd = got[:, 1, c * 8:c * 8 + 8]
            m = lower[None]
            for k in range(2):
                rows = jnp.where(m, even, odd) if k == 0 else jnp.where(m, odd, even)
                high, low = split(rows.reshape(256, LANES))
                nh, nl = narrow[k, 0, part], narrow[k, 1, part]
                term = mul(nh, high, NN) + mul(nh, low, NN) + mul(nl, high, NN)
                acc[c, k] = jnp.where(part == 0, term, acc[c, k] + term)
        return carry

    acc[...] = jnp.zeros_like(acc)
    lax.fori_loop(0, PARTS, narrow_part, 0)

    for c in range(2):
        for k in range(2):
            full = jnp.transpose(acc[c, k])
            own[0, c, k] = full[:64]
            own[1, c, k] = full[64:]
    swap2 = pltpu.make_async_remote_copy(
        src_ref=own.at[1 - core], dst_ref=res_recv, send_sem=s_swap.at[2], recv_sem=s_swap.at[3],
        device_id=buddy, device_id_type=MESH)
    swap2.start()

    span = far_recv.at[pl.ds(0, 7)]
    pltpu.make_async_copy(span, span, s_far.at[1]).wait()
    for c in range(2):
        for k in range(2):
            for g in range(8):
                rows = slice(g * 8, g * 8 + 8)
                out[core, c, k, rows, :] = own[core, c, k, rows, :] + far_recv[g, core, c, k]
    swap2.wait()
    for c in range(2):
        for k in range(2):
            for g in range(8):
                rows = slice(g * 8, g * 8 + 8)
                out[1 - core, c, k, rows, :] = res_recv[c, k, rows, :] + far_recv[g, 1 - core, c, k]

    def sent(part, carry):
        wait_all(part, send1, s_main.at[0, part])
        wait_all(part, send2, s_back.at[0, part])
        return carry

    lax.fori_loop(0, PARTS, sent, 0)
    span = child_recv.at[pl.ds(0, 7)]
    pltpu.make_async_copy(span, span, s_child.at[0]).wait()
    span = far_out.at[pl.ds(0, 7)]
    pltpu.make_async_copy(span, span, s_far.at[0]).wait()
    span = tab_in.at[pl.ds(0, 7)]
    pltpu.make_async_copy(span, span, s_tab.at[0]).wait()


def shards(child_rad, box_at_slot, octant, far_par, far_par_off, far_child, far_child_off, far_child_count,
           trans_par, trans_child):
    b = lax.axis_index("box")
    x = jnp.transpose(child_rad, (3, 2, 1, 0, 4))
    x = jnp.pad(x, ((0, 0),) * 3 + ((0, 6), (0, 0))).reshape(2, 2, 2, 8, 7, T_CHILD)
    x = jnp.pad(x, ((0, 0),) * 4 + ((0, 1), (0, 0))).reshape(2, 2, 2, 64, T_CHILD)
    t = lax.dynamic_slice_in_dim(trans_par, 96 * b, 96, 3).reshape(100, 8, 2, 8, PARTS, 4)
    t = jnp.transpose(t, (3, 4, 1, 2, 5, 0))
    t = jnp.pad(t, ((0, 0),) * 5 + ((0, LANES - 100),)).reshape(8, PARTS, 8, 8, LANES)
    tc = lax.dynamic_slice_in_dim(trans_child, jnp.minimum(GROUP * b, 42), 8, 0)
    tc = jnp.where(b == 7, tc[7:8], tc)
    tc = jnp.transpose(tc, (1, 2, 0, 3))

    wide, narrow = theta_tables()
    vmem = pl.BlockSpec(memory_space=pltpu.VMEM)
    smem = pl.BlockSpec(memory_space=pltpu.SMEM)
    out = pl.pallas_call(
        kernel,
        out_shape=jax.ShapeDtypeStruct((2, 2, 2, 64, T_CHILD), F32),
        in_specs=[smem] * 7 + [vmem] * 7,
        out_specs=vmem,
        scratch_shapes=[
            pltpu.SMEM((8,), jnp.int32),
            pltpu.SMEM((8,), jnp.int32),
            pltpu.SMEM((8,), jnp.int32),
            pltpu.SMEM((24,), jnp.int32),
            pltpu.SMEM((24,), jnp.int32),
            pltpu.SMEM((112,), jnp.int32),
            pltpu.SMEM((112,), jnp.int32),
            pltpu.SMEM((112,), jnp.int32),
            pltpu.SMEM((112,), F32),
            pltpu.VMEM((2, 2, 64, T_CHILD), F32),
            pltpu.VMEM((2, 2, 128, T_CHILD), BF16),
            pltpu.VMEM((2, 2, 128, T_CHILD), BF16),
            pltpu.VMEM((PARTS, 64, 16, LANES), F32),
            pltpu.VMEM((PARTS, 64, 16, LANES), F32),
            pltpu.VMEM((PARTS, 64, 16, LANES), F32),
            pltpu.VMEM((PARTS, 64, 16, LANES), F32),
            pltpu.VMEM((8, 2, 2, 2, 8, T_CHILD), F32),
            pltpu.VMEM((8, 2, 2, 2, 8, T_CHILD), F32),
            pltpu.VMEM((8, 2, 2, 2, 8, T_CHILD), F32),
            pltpu.VMEM((2, 8, PARTS, 8, 8, LANES), F32),
            pltpu.VMEM((8, 2, 8, 16 * LANES), F32),
            pltpu.VMEM((8, 2, 8, 16 * LANES), F32),
            pltpu.VMEM((2, 128, 8 * LANES), F32),
            pltpu.VMEM((2, 8, 2, 8, LANES), F32),
            pltpu.VMEM((2, 128, 8 * LANES), BF16),
            pltpu.VMEM((2, 128, 8 * LANES), BF16),
            pltpu.VMEM((2, 2, T_CHILD, LANES), F32),
            pltpu.VMEM((2, 2, 2, 64, T_CHILD), F32),
            pltpu.VMEM((2, 2, 64, T_CHILD), F32),
            pltpu.SemaphoreType.DMA((4,)),
            pltpu.SemaphoreType.DMA((2,)),
            pltpu.SemaphoreType.DMA((2,)),
            pltpu.SemaphoreType.DMA((2,)),
            pltpu.SemaphoreType.DMA((2,)),
            pltpu.SemaphoreType.DMA((2, PARTS)),
            pltpu.SemaphoreType.DMA((2, PARTS)),
            pltpu.SemaphoreType.DMA((2,)),
        ],
        compiler_params=pltpu.CompilerParams(
            collective_id=0, has_side_effects=True, vmem_limit_bytes=56 * 2**20),
        cost_estimate=pl.CostEstimate(flops=14_000_000_000, bytes_accessed=16_000_000, transcendentals=0),
        name="fields",
    )(box_at_slot, octant, far_par, far_par_off, far_child, far_child_off, far_child_count,
      x, t, tc, jnp.asarray(wide), jnp.asarray(narrow), jnp.asarray(phi_tables()), jnp.asarray(phi_angles()))
    out = out.reshape(2, 2, 2, 8, 8, T_CHILD)[:, :, :, :, :GROUP].reshape(2, 2, 2, 56, T_CHILD)[:, :, :, :50]
    return jnp.transpose(out, (3, 2, 1, 0, 4))


def solution(mesh):
    return jax.shard_map(
        shards,
        mesh=mesh,
        in_specs=(P("dir", "box", None, None, None), P(), P(), P(), P(), P(), P(), P(),
                  P("dir", None, None, None), P("dir", None, None, None)),
        out_specs=P("dir", "box", None, None, None),
        check_vma=False,
    )
```

```python
import functools
import math

import jax
import jax.numpy as jnp
import numpy as np
from jax import lax
from jax.experimental import pallas as pl
from jax.experimental.pallas import tpu as pltpu
from jax.sharding import PartitionSpec as P

T_CHILD, P_CHILD = 384, 800
T_PARENT, P_PARENT = 768, 1600
FAR_P, FAR_C = 3, 7

PARTS = 3
LANES = 128
GROUP = 7
MESH = pl.DeviceIdType.MESH
F32, BF16 = jnp.float32, jnp.bfloat16


def split_np(table):
    high = table.astype(np.float32).astype(jnp.bfloat16)
    low = (table - high.astype(np.float64)).astype(np.float32).astype(jnp.bfloat16)
    return high, low


@functools.cache
def theta_tables():
    q = np.arange(T_PARENT)
    first = np.clip((q - 1) // 2 - 2, 0, T_CHILD - 6)
    offset = q * 0.5 - 0.25 - first
    table = np.zeros((T_PARENT, T_CHILD))
    for node in range(6):
        weight = np.ones(T_PARENT)
        for other in range(6):
            if other != node:
                weight = weight * (offset - other) / (node - other)
        table[q, first + node] = weight
    part, pair, place, i = np.meshgrid(np.arange(PARTS), np.arange(32), np.arange(2), np.arange(4), indexing="ij")
    wide, narrow = [], []
    for kid in range(2):
        chip = 2 * pair + (place if kid == 0 else 1 - place)
        rows = table[(12 * chip + 4 * part + i).reshape(-1)]
        wide.append(np.stack(split_np(rows)))
        back = 0.25 * rows.reshape(PARTS, 256, T_CHILD).transpose(0, 2, 1)
        narrow.append(np.stack(split_np(back)))
    return np.stack(wide), np.stack(narrow)


@functools.cache
def phi_tables():
    p = np.arange(P_PARENT)[:, None]
    c = np.arange(P_CHILD)[None, :]
    odd = 2 * p - 4 * c - 1
    period = 4 * P_CHILD
    numerator = np.mod((P_CHILD - 1) * odd, 2 * period).astype(np.float64)
    table = np.sin(math.pi * numerator / period) / (P_CHILD * np.sin(math.pi * odd / period))
    plus = np.zeros((4 * LANES, 8 * LANES))
    minus = np.zeros((4 * LANES, 8 * LANES))
    f = np.arange(50)
    for jj in range(4):
        for core in range(2):
            child = 100 * jj + 50 * core + f
            rows = jj * LANES + core * 50 + f
            for dd in range(8):
                parent = 100 * dd + np.arange(100)
                near = table[np.ix_(parent, child)].T
                far = table[np.ix_(parent, child + 400)].T
                at = np.ix_(rows, dd * LANES + np.arange(100))
                plus[at] = 0.5 * (near + far)
                minus[at] = 0.5 * (near - far)
    return np.stack([np.stack(split_np(plus)), np.stack(split_np(minus))])


@functools.cache
def phi_angles():
    lane = np.arange(16 * LANES)
    phi = 2.0 * math.pi * (100 * (lane // LANES) + lane % LANES + 0.5) / P_PARENT
    return np.stack([np.cos(phi), np.sin(phi)]).reshape(2, 1, 16 * LANES).astype(np.float32)


def split(x):
    high = x.astype(BF16)
    return high, (x - high.astype(F32)).astype(BF16)


NT = (((1,), (1,)), ((), ()))
NN = (((1,), (0,)), ((), ()))


def mul(a, b, dims):
    return lax.dot_general(a, b, dims, preferred_element_type=F32)


def kernel(
    bas, octant, far_par, far_par_off, far_child, far_child_off, far_count,
    x_hbm, tab_hbm, tabc_hbm, wide_hbm, narrow_hbm, weights_hbm, angles,
    out,
    slot_of, oct_lo, oct_hi, par_src, par_off, kid_src, kid_kid, kid_off, kid_act,
    x_raw, tab_raw, tabc_raw, wide, narrow, weights,
    xf, x_swap, x_hi, x_lo, send1, recv1, send2, recv2,
    child_recv, child, tabc, far_out, far_recv, far, tv, tab_send, tab_recv, tab, etab, y, pr, r_hi, r_lo, acc, own,
    res_recv,
    s_in, s_swap, s_child, s_far, s_tab, s_tabf, s_main, s_back, s_loc,
):
    b = lax.axis_index("box")
    d = lax.axis_index("dir")
    core = lax.rem(d, 2)
    j = d // 2
    me = b * 8 + j
    chip_odd = lax.rem(j, 2) == 1
    buddy = (b, d + 1 - 2 * core)

    def chip(t):
        return (t // 8, lax.rem(t, 8) * 2 + core)

    barrier = pltpu.get_barrier_semaphore()
    pl.semaphore_signal(barrier, inc=1, device_id=buddy, device_id_type=MESH)

    def greet(i, carry):
        pl.semaphore_signal(barrier, inc=1, device_id=chip(lax.rem(me + i, 64)), device_id_type=MESH)
        return carry

    group = jnp.minimum(GROUP * b, 50 - GROUP)
    window = pl.multiple_of((3 * (b // 2)) // 2 * LANES, LANES)
    loads = [
        pltpu.make_async_copy(x_hbm, x_raw, s_in.at[0]),
        pltpu.make_async_copy(wide_hbm, wide, s_in.at[1]),
        pltpu.make_async_copy(tab_hbm.at[:, :, :, pl.ds(window, 256)], tab_raw, s_in.at[2]),
        pltpu.make_async_copy(tabc_hbm.at[pl.ds(group, GROUP)], tabc_raw, s_in.at[3]),
        pltpu.make_async_copy(weights_hbm, weights, s_in.at[4]),
        pltpu.make_async_copy(narrow_hbm, narrow, s_in.at[5]),
    ]
    loads[0].start()
    lax.fori_loop(1, 64, greet, 0)
    for load in loads[1:]:
        load.start()

    for box in range(8):
        place = jnp.int32(0)
        for s in range(8):
            place = jnp.where(bas[s] == box, s, place)
        slot_of[box] = place
    for s in range(8):
        box = bas[s]
        o0, o1 = octant[2 * box], octant[2 * box + 1]
        oct_lo[s] = jnp.where(chip_odd, o1, o0)
        oct_hi[s] = jnp.where(chip_odd, o0, o1)
        for k in range(FAR_P):
            par_src[s * FAR_P + k] = slot_of[far_par[k, box]]
            par_off[s * FAR_P + k] = far_par_off[k, box]

    def kid_entry(n, carry):
        box = bas[n // 2] * 2 + lax.rem(n, 2)
        for k in range(FAR_C):
            source = far_child[k, box]
            kid_src[n * FAR_C + k] = slot_of[source // 2]
            kid_kid[n * FAR_C + k] = lax.rem(source, 2)
            kid_off[n * FAR_C + k] = far_child_off[k, box]
            kid_act[n * FAR_C + k] = jnp.where(k < far_count[box], 1.0, 0.0).astype(F32)
        return carry

    loads[0].wait()
    for p in range(2):
        for c in range(2):
            for k in range(2):
                xf[p, c, k, 0:50, :] = x_raw[:, k, c, p, :]

    pl.semaphore_wait(barrier, 64)

    swap = pltpu.make_async_remote_copy(
        src_ref=xf.at[1 - core], dst_ref=x_swap, send_sem=s_swap.at[0], recv_sem=s_swap.at[1],
        device_id=buddy, device_id_type=MESH)
    swap.start()

    def child_start(i, carry):
        g = lax.rem(b + i, 8)
        pltpu.make_async_remote_copy(
            src_ref=x_raw.at[pl.ds(jnp.minimum(GROUP * g, 50 - GROUP), GROUP)], dst_ref=child_recv.at[b],
            send_sem=s_child.at[0], recv_sem=s_child.at[1], device_id=(g, d), device_id_type=MESH).start()
        return carry

    lax.fori_loop(1, 8, child_start, 0)
    child_own = pltpu.make_async_copy(x_raw.at[pl.ds(group, GROUP)], child_recv.at[b], s_loc.at[0])
    child_own.start()

    lax.fori_loop(0, 16, kid_entry, 0)

    lower = lax.broadcasted_iota(jnp.int32, (8, LANES), 0) < 4
    lane = lax.broadcasted_iota(jnp.int32, (8, LANES), 1)

    y_hi, x_at = j // 4, lax.rem(j, 4)
    other_box = b + 1 - 2 * lax.rem(b, 2)
    first_chip = [b * 8 + y_hi * 4, other_box * 8 + (1 - y_hi) * 4]
    rows = lax.broadcasted_iota(jnp.int32, (96, 256), 0)
    columns = lax.broadcasted_iota(jnp.int32, (96, 256), 1)
    sets = (rows >= 48).astype(jnp.int32)
    parts = (rows >> 4) - 3 * sets
    place = (rows >> 2) & 3
    theta_at = 12 * (jnp.where(rows >= 48, first_chip[1], first_chip[0]) + place) + 4 * parts + (rows & 3) - window
    swapped = theta_at + jnp.where((place & 1) == 0, 12, -12)
    picks = [(columns == q).astype(F32).astype(BF16) for q in (theta_at, swapped)]
    loads[2].wait()
    tv[...] = jnp.zeros_like(tv)

    def tab_prepare(off, carry):
        got = []
        for c in range(2):
            tv[c, 0:100, :] = tab_raw[:, off, c, :]
            high, low = split(tv[c])
            got.append((mul(picks[c], high, NT) + mul(picks[c], low, NT)).reshape(2, 3, 2, 2, 4, LANES))
        flat = [g.reshape(12, 8, LANES) for g in got]
        even = jnp.where(lower[None], flat[0], flat[1]).reshape(2, 3, 2, 8, LANES)
        odd = jnp.where(lower[None], flat[1], flat[0]).reshape(2, 3, 2, 8, LANES)
        for s in range(2):
            for u in range(2):
                tab_send[s, 2 * u, :, off] = even[s, :, u]
                tab_send[s, 2 * u + 1, :, off] = odd[s, :, u]
        return carry

    lax.fori_loop(0, 8, tab_prepare, 0)

    def tab_start(x, carry):
        def go(s):
            box = b if s == 0 else other_box
            half = y_hi if s == 0 else 1 - y_hi
            pltpu.make_async_remote_copy(
                src_ref=tab_send.at[s, x], dst_ref=tab_recv.at[core, j], send_sem=s_tab.at[0], recv_sem=s_tab.at[1],
                device_id=(box, (half * 4 + x) * 2 + core), device_id_type=MESH).start()

        go(1)

        @pl.when(x != x_at)
        def _():
            go(0)

        return carry

    lax.fori_loop(0, 4, tab_start, 0)
    tab_recv[core, j] = tab_send[0, x_at]

    swap.wait()

    def gather_rows(c, carry):
        for k in range(2):
            mine, other = xf[core, c, k, 0:50, :], x_swap[c, k, 0:50, :]
            zero = core == 0
            full = jnp.concatenate(
                [jnp.where(zero, mine, other), jnp.where(zero, other, mine), jnp.zeros((28, T_CHILD), F32)], axis=0)
            high, low = split(full)
            x_hi[c, k] = high
            x_lo[c, k] = low
        return carry

    lax.fori_loop(0, 2, gather_rows, 0)
    loads[1].wait()

    def send_all(part, count, send, recv, sems):
        def start(i, carry):
            t = lax.rem(me + i, 64)
            pltpu.make_async_remote_copy(
                src_ref=send.at[part, t, pl.ds(0, count)], dst_ref=recv.at[part, me, pl.ds(0, count)],
                send_sem=sems.at[0, part], recv_sem=sems.at[1, part], device_id=chip(t), device_id_type=MESH).start()
            return carry

        lax.fori_loop(1, 64, start, 0)
        recv[part, me] = send[part, me]

    def wait_all(part, count, ref, sem):
        span = ref.at[part, pl.ds(0, 63), pl.ds(0, count)]
        pltpu.make_async_copy(span, span, sem).wait()

    spare = (lane >= 100) & (lane < 125)

    def stow(m, tile, extra):
        shape = tile.shape
        moved = pltpu.roll(extra.reshape(-1, LANES), 100 - 25 * m, 1).reshape(shape)
        return jnp.where(spare[None], moved, tile)

    def unstow(m, tile, extra):
        shape = tile.shape
        moved = pltpu.roll(tile.reshape(-1, LANES), 28 + 25 * m, 1).reshape(shape)
        return jnp.where(((lane >= 25 * m) & (lane < 25 * m + 25))[None], moved, extra)

    def widen(part, carry):
        rows = pl.ds(pl.multiple_of(part * 256, 256), 256)
        for c in range(2):
            got = []
            for k in range(2):
                hi, lo = x_hi[c, k], x_lo[c, k]
                th, tl = wide[k, 0, rows, :], wide[k, 1, rows, :]
                got.append(mul(th, hi, NT) + mul(th, lo, NT) + mul(tl, hi, NT))
            k0 = got[0].reshape(32, 8, LANES)
            k1 = got[1].reshape(32, 8, LANES)
            m = lower[None]
            even = jnp.where(m, k0, k1)
            odd = jnp.where(m, k1, k0)
            both = jnp.stack([even, odd], axis=1).reshape(64, 8, LANES)
            send1[part, :, c * 8:c * 8 + 8, :] = both
        return carry

    lax.fori_loop(0, PARTS, widen, 0)

    def stow_forward(i, carry):
        at = pl.ds(i * 8, 8)
        extra = send1[2, at, 8:16, :]
        for m in range(4):
            half = slice(8 * (m % 2), 8 * (m % 2) + 8)
            send1[m // 2, at, half, :] = stow(m, send1[m // 2, at, half, :], extra)
        return carry

    lax.fori_loop(0, 8, stow_forward, 0)

    def send_forward(part, carry):
        send_all(part, 16, send1, recv1, s_main)
        return carry

    lax.fori_loop(0, 2, send_forward, 0)
    send_all(2, 8, send1, recv1, s_main)

    loads[3].wait()
    for off in range(16):
        for c in range(2):
            tabc[off, c, 0:GROUP, :] = tabc_raw[:, off, c, :]
    child_own.wait()
    span = child_recv.at[pl.ds(0, 7)]
    pltpu.make_async_copy(span, span, s_child.at[1]).wait()

    def child_rows(src, carry):
        for p in range(2):
            for c in range(2):
                for k in range(2):
                    child[src, p, c, k, 0:GROUP, :] = child_recv[src, :, k, c, p, :]
        return carry

    lax.fori_loop(0, 8, child_rows, 0)

    def far_slot(s, carry):
        for kid in range(2):
            n = s * 2 + kid
            total = [[jnp.zeros((GROUP, T_CHILD), F32) for _ in range(2)] for _ in range(2)]
            for k in range(FAR_C):
                src, sk, off = kid_src[n * FAR_C + k], kid_kid[n * FAR_C + k], kid_off[n * FAR_C + k]
                act = kid_act[n * FAR_C + k]
                tr, ti = tabc[off, 0, 0:GROUP, :] * act, tabc[off, 1, 0:GROUP, :] * act
                for p in range(2):
                    xr, xi = child[src, p, 0, sk, 0:GROUP, :], child[src, p, 1, sk, 0:GROUP, :]
                    total[p][0] = total[p][0] + (tr * xr - ti * xi)
                    total[p][1] = total[p][1] + (tr * xi + ti * xr)
            for p in range(2):
                for c in range(2):
                    far_out[s, 0:GROUP, kid, c, p, :] = total[p][c]
        return carry

    lax.fori_loop(0, 8, far_slot, 0)

    far_row = jnp.where(b == 7, GROUP - 1, 0)

    def far_start(i, carry):
        to = lax.rem(b + i, 8)
        pltpu.make_async_remote_copy(
            src_ref=far_out.at[to, pl.ds(far_row, GROUP)], dst_ref=far_recv.at[b],
            send_sem=s_far.at[0], recv_sem=s_far.at[1], device_id=(to, d), device_id_type=MESH).start()
        return carry

    lax.fori_loop(1, 8, far_start, 0)
    far_own = pltpu.make_async_copy(far_out.at[b, pl.ds(far_row, GROUP)], far_recv.at[b], s_loc.at[1])
    far_own.start()

    span = tab_recv.at[core, pl.ds(0, 7)]
    pltpu.make_async_copy(span, span, s_tab.at[1]).wait()
    tab_on = pltpu.make_async_remote_copy(
        src_ref=tab_recv.at[core], dst_ref=tab_recv.at[core], send_sem=s_tabf.at[0], recv_sem=s_tabf.at[1],
        device_id=buddy, device_id_type=MESH)
    tab_on.start()
    loads[4].wait()
    tab_on.wait()

    row = lax.broadcasted_iota(jnp.int32, (8, LANES), 0)

    def one_part(part, carry):
        q = (12 * me + 4 * part + lax.rem(row, 4)).astype(F32)
        theta = (q + 0.5) * (math.pi / T_PARENT)
        st, ct = 16.0 * jnp.sin(theta), 16.0 * jnp.cos(theta)

        def prepare(blk, carry):
            at = pl.ds(pl.multiple_of(blk * LANES, LANES), LANES)
            ux, uy = st * angles[0, :, at], st * angles[1, :, at]
            for o in range(4):
                t = ct + (ux if o % 2 else -ux) + (uy if o // 2 else -uy)
                f = t - jnp.round(t)
                a = f * f
                s = f * (3.14159265358979 + a * (-5.16771278004997 + a * (2.55016403987735 + a * (
                    -0.599264529320792 + a * (0.0821458866111282 + a * (-0.00737043094571435
                    + a * 0.000466302805767613))))))
                c = 1.0 + a * (-4.93480220054468 + a * (4.05871212641677 + a * (-1.33526276885459 + a * (
                    0.235330630358893 + a * (-0.0258068913900141 + a * (0.00192957430940392
                    - a * 0.000104638104924846))))))
                cos, sin = 1.0 - 2.0 * (s * s), 2.0 * (s * c)
                etab[4 + o, 0, :, at] = cos
                etab[4 + o, 1, :, at] = sin
                etab[3 - o, 0, :, at] = cos
                etab[3 - o, 1, :, at] = -sin
            dcore, dj = lax.rem(blk, 2), blk // 2
            for off in range(8):
                v = tab_recv[dcore, dj, part, off]
                w = pltpu.roll(v, 4, 0)
                one = jnp.where(lower, v, w)
                two = jnp.where(lower, w, v)
                tab[off, 0, :, at] = jnp.where(chip_odd, two, one)
                tab[off, 1, :, at] = jnp.where(chip_odd, one, two)
            return carry

        lax.fori_loop(0, 16, prepare, 0)

        @pl.when(part < 2)
        def _():
            wait_all(part, 16, recv1, s_main.at[1, part])

        @pl.when(part == 2)
        def _():
            wait_all(2, 8, recv1, s_main.at[1, 2])

            def take(i, carry):
                at = pl.ds(i * 8, 8)
                extra = jnp.zeros((8, 8, LANES), F32)
                for m in range(4):
                    extra = unstow(m, recv1[m // 2, at, 8 * (m % 2):8 * (m % 2) + 8, :], extra)
                recv1[2, at, 8:16, :] = extra
                return carry

            lax.fori_loop(0, 8, take, 0)

        got = recv1[part].reshape(8, 8, 16, LANES)
        for sign in range(2):
            pieces = []
            for jj in range(4):
                one, two = got[:, jj], got[:, jj + 4]
                pieces.append((one + two if sign == 0 else one - two).reshape(128, LANES))
            high, low = split(jnp.concatenate(pieces, axis=1))
            for n in range(4):
                cols = slice(n * 256, n * 256 + 256)
                wh, wl = weights[sign, 0, :, cols], weights[sign, 1, :, cols]
                y[sign, :, cols] = mul(high, wh, NN) + mul(low, wh, NN) + mul(high, wl, NN)

        def block(dd, carry):
            for half in range(2):
                at_y = pl.ds(pl.multiple_of(dd * LANES, LANES), LANES)
                at = pl.ds(pl.multiple_of((dd + 8 * half) * LANES, LANES), LANES)
                for s in range(8):
                    yp = y[0, s * 16:s * 16 + 16, at_y]
                    ym = y[1, s * 16:s * 16 + 16, at_y]
                    v = yp + ym if half == 0 else yp - ym
                    vr, vi = v[:8], v[8:]
                    cos = jnp.where(lower, etab[oct_lo[s], 0, :, at], etab[oct_hi[s], 0, :, at])
                    sin = jnp.where(lower, etab[oct_lo[s], 1, :, at], etab[oct_hi[s], 1, :, at])
                    re = cos * vr - sin * vi
                    im = sin * vr + cos * vi
                    pr[half, s, 0] = re + pltpu.roll(re, 4, 0)
                    pr[half, s, 1] = im + pltpu.roll(im, 4, 0)
            for s in range(8):
                back = []
                for half in range(2):
                    at = pl.ds(pl.multiple_of((dd + 8 * half) * LANES, LANES), LANES)
                    re = im = None
                    for k in range(FAR_P):
                        src, off = par_src[s * FAR_P + k], par_off[s * FAR_P + k]
                        fr, fi = pr[half, src, 0], pr[half, src, 1]
                        tr, ti = tab[off, 0, :, at], tab[off, 1, :, at]
                        gr, gi = tr * fr - ti * fi, tr * fi + ti * fr
                        re = gr if re is None else re + gr
                        im = gi if im is None else im + gi
                    cos = jnp.where(lower, etab[oct_lo[s], 0, :, at], etab[oct_hi[s], 0, :, at])
                    sin = jnp.where(lower, etab[oct_lo[s], 1, :, at], etab[oct_hi[s], 1, :, at])
                    back.append(jnp.concatenate([cos * re + sin * im, cos * im - sin * re], axis=0))
                at_y = pl.ds(pl.multiple_of(dd * LANES, LANES), LANES)
                for sign in range(2):
                    high, low = split(back[0] + back[1] if sign == 0 else back[0] - back[1])
                    r_hi[sign, s * 16:s * 16 + 16, at_y] = high
                    r_lo[sign, s * 16:s * 16 + 16, at_y] = low
            return carry

        lax.fori_loop(0, 8, block, 0)

        z = []
        for sign in range(2):
            high, low = r_hi[sign], r_lo[sign]
            wh, wl = weights[sign, 0], weights[sign, 1]
            z.append(mul(high, wh, NT) + mul(low, wh, NT) + mul(high, wl, NT))
        one, two = z[0] + z[1], z[0] - z[1]
        for jj in range(4):
            cols = slice(jj * LANES, jj * LANES + LANES)
            a = one[:, cols].reshape(8, 16, LANES)
            c = two[:, cols].reshape(8, 16, LANES)
            for s in range(8):
                send2[part, s * 8 + jj] = a[s]
                send2[part, s * 8 + jj + 4] = c[s]

        for at_part in range(PARTS):
            @pl.when(part == at_part)
            def _():
                if at_part > 0:
                    def stow_back(i, carry):
                        at = pl.ds(i * 8, 8)
                        extra = send2[0, at, 8:16, :]
                        for h in range(2):
                            half = slice(8 * h, 8 * h + 8)
                            send2[at_part, at, half, :] = stow(
                                2 * at_part - 2 + h, send2[at_part, at, half, :], extra)
                        return carry

                    lax.fori_loop(0, 8, stow_back, 0)
                send_all(at_part, 16 if at_part > 0 else 8, send2, recv2, s_back)

        return carry

    lax.fori_loop(0, PARTS, one_part, 0)

    far_own.wait()
    span = far_recv.at[pl.ds(0, 7)]
    pltpu.make_async_copy(span, span, s_far.at[1]).wait()
    for p in range(2):
        for c in range(2):
            for k in range(2):
                for g in range(8):
                    count = GROUP if g < 7 else 1
                    far[p, c, k, g * GROUP:g * GROUP + count, :] = far_recv[g, 0:count, k, c, p, :]

    loads[5].wait()
    acc[...] = jnp.zeros_like(acc)

    def narrow_tile(part, c):
        got = recv2[part, :, c * 8:c * 8 + 8, :].reshape(32, 2, 8, LANES)
        even, odd = got[:, 0], got[:, 1]
        m = lower[None]
        for k in range(2):
            rows = jnp.where(m, even, odd) if k == 0 else jnp.where(m, odd, even)
            high, low = split(rows.reshape(256, LANES))
            nh, nl = narrow[k, 0, part], narrow[k, 1, part]
            acc[c, k] = acc[c, k] + (mul(nh, high, NN) + mul(nh, low, NN) + mul(nl, high, NN))

    wait_all(0, 8, recv2, s_back.at[1, 0])
    narrow_tile(0, 0)

    def narrow_part(part, carry):
        wait_all(part, 16, recv2, s_back.at[1, part])
        for c in range(2):
            narrow_tile(part, c)
        return carry

    lax.fori_loop(1, PARTS, narrow_part, 0)

    def take_back(i, carry):
        at = pl.ds(i * 8, 8)
        extra = jnp.zeros((8, 8, LANES), F32)
        for m in range(4):
            extra = unstow(m, recv2[1 + m // 2, at, 8 * (m % 2):8 * (m % 2) + 8, :], extra)
        recv2[0, at, 8:16, :] = extra
        return carry

    lax.fori_loop(0, 8, take_back, 0)
    narrow_tile(0, 1)

    for c in range(2):
        for k in range(2):
            full = jnp.transpose(acc[c, k])
            own[0, c, k, 0:50, :] = full[0:50]
            own[1, c, k, 0:50, :] = full[50:100]
    swap2 = pltpu.make_async_remote_copy(
        src_ref=own.at[1 - core], dst_ref=res_recv, send_sem=s_swap.at[2], recv_sem=s_swap.at[3],
        device_id=buddy, device_id_type=MESH)
    swap2.start()
    for p in range(2):
        @pl.when(core == p)
        def _():
            for c in range(2):
                for k in range(2):
                    out[:, k, c, p, :] = own[p, c, k, 0:50, :] + far[p, c, k, 0:50, :]

    swap2.wait()
    for p in range(2):
        @pl.when(core != p)
        def _():
            for c in range(2):
                for k in range(2):
                    out[:, k, c, p, :] = res_recv[c, k, 0:50, :] + far[p, c, k, 0:50, :]

    for part in range(PARTS):
        wait_all(part, 8 if part == 2 else 16, send1, s_main.at[0, part])
        wait_all(part, 8 if part == 0 else 16, send2, s_back.at[0, part])
    span = child_recv.at[pl.ds(0, 7)]
    pltpu.make_async_copy(span, span, s_child.at[0]).wait()
    span = far_recv.at[pl.ds(0, 7)]
    pltpu.make_async_copy(span, span, s_far.at[0]).wait()
    span = tab_recv.at[core, pl.ds(0, 7)]
    pltpu.make_async_copy(span, span, s_tab.at[0]).wait()


def shards(child_rad, box_at_slot, octant, far_par, far_par_off, far_child, far_child_off, far_child_count,
           trans_par, trans_child):
    wide, narrow = theta_tables()
    vmem = pl.BlockSpec(memory_space=pltpu.VMEM)
    smem = pl.BlockSpec(memory_space=pltpu.SMEM)
    anywhere = pl.BlockSpec(memory_space=pl.ANY)
    chunks = pltpu.VMEM((PARTS, 64, 16, LANES), F32)
    groups = pltpu.VMEM((8, GROUP, 2, 2, 2, T_CHILD), F32)
    return pl.pallas_call(
        kernel,
        out_shape=jax.ShapeDtypeStruct((50, 2, 2, 2, T_CHILD), F32),
        in_specs=[smem] * 7 + [anywhere] * 6 + [vmem],
        out_specs=vmem,
        scratch_shapes=[
            pltpu.SMEM((8,), jnp.int32),
            pltpu.SMEM((8,), jnp.int32),
            pltpu.SMEM((8,), jnp.int32),
            pltpu.SMEM((24,), jnp.int32),
            pltpu.SMEM((24,), jnp.int32),
            pltpu.SMEM((112,), jnp.int32),
            pltpu.SMEM((112,), jnp.int32),
            pltpu.SMEM((112,), jnp.int32),
            pltpu.SMEM((112,), F32),
            pltpu.VMEM((50, 2, 2, 2, T_CHILD), F32),
            pltpu.VMEM((100, 8, 2, 256), F32),
            pltpu.VMEM((GROUP, 16, 2, T_CHILD), F32),
            pltpu.VMEM(wide.shape, BF16),
            pltpu.VMEM(narrow.shape, BF16),
            pltpu.VMEM((2, 2, 4 * LANES, 8 * LANES), BF16),
            pltpu.VMEM((2, 2, 2, 56, T_CHILD), F32),
            pltpu.VMEM((2, 2, 56, T_CHILD), F32),
            pltpu.VMEM((2, 2, 128, T_CHILD), BF16),
            pltpu.VMEM((2, 2, 128, T_CHILD), BF16),
            chunks, chunks, chunks, chunks,
            groups,
            pltpu.VMEM((8, 2, 2, 2, 8, T_CHILD), F32),
            pltpu.VMEM((16, 2, 8, T_CHILD), F32),
            pltpu.VMEM((8, 2 * GROUP - 1, 2, 2, 2, T_CHILD), F32),
            groups,
            pltpu.VMEM((2, 2, 2, 56, T_CHILD), F32),
            pltpu.VMEM((2, LANES, 256), F32),
            pltpu.VMEM((2, 4, PARTS, 8, 8, LANES), F32),
            pltpu.VMEM((2, 8, PARTS, 8, 8, LANES), F32),
            pltpu.VMEM((8, 2, 8, 16 * LANES), F32),
            pltpu.VMEM((8, 2, 8, 16 * LANES), F32),
            pltpu.VMEM((2, 128, 8 * LANES), F32),
            pltpu.VMEM((2, 8, 2, 8, LANES), F32),
            pltpu.VMEM((2, 128, 8 * LANES), BF16),
            pltpu.VMEM((2, 128, 8 * LANES), BF16),
            pltpu.VMEM((2, 2, T_CHILD, LANES), F32),
            pltpu.VMEM((2, 2, 2, 56, T_CHILD), F32),
            pltpu.VMEM((2, 2, 56, T_CHILD), F32),
            pltpu.SemaphoreType.DMA((6,)),
            pltpu.SemaphoreType.DMA((4,)),
            pltpu.SemaphoreType.DMA((2,)),
            pltpu.SemaphoreType.DMA((2,)),
            pltpu.SemaphoreType.DMA((2,)),
            pltpu.SemaphoreType.DMA((2,)),
            pltpu.SemaphoreType.DMA((2, PARTS)),
            pltpu.SemaphoreType.DMA((2, PARTS)),
            pltpu.SemaphoreType.DMA((2,)),
        ],
        compiler_params=pltpu.CompilerParams(
            collective_id=0, has_side_effects=True, vmem_limit_bytes=60 * 2**20),
        cost_estimate=pl.CostEstimate(flops=14_000_000_000, bytes_accessed=16_000_000, transcendentals=0),
        name="fields",
    )(box_at_slot, octant, far_par.T, far_par_off.T, far_child.T, far_child_off.T, far_child_count,
      child_rad, trans_par, trans_child,
      jnp.asarray(wide), jnp.asarray(narrow), jnp.asarray(phi_tables()), jnp.asarray(phi_angles()))


def solution(mesh):
    return jax.shard_map(
        shards,
        mesh=mesh,
        in_specs=(P("dir", "box", None, None, None), P(), P(), P(), P(), P(), P(), P(),
                  P("dir", None, None, None), P("dir", None, None, None)),
        out_specs=P("dir", "box", None, None, None),
        check_vma=False,
    )
```

```python
import functools
import math

import jax
import jax.numpy as jnp
import numpy as np
from jax import lax
from jax.experimental import pallas as pl
from jax.experimental.pallas import tpu as pltpu
from jax.sharding import PartitionSpec as P

T_CHILD, P_CHILD = 384, 800
T_PARENT, P_PARENT = 768, 1600
FAR_P, FAR_C = 3, 7

PARTS = 3
LANES = 128
GROUP = 7
MESH = pl.DeviceIdType.MESH
F32, BF16 = jnp.float32, jnp.bfloat16


def split_np(table):
    high = table.astype(np.float32).astype(jnp.bfloat16)
    low = (table - high.astype(np.float64)).astype(np.float32).astype(jnp.bfloat16)
    return high, low


@functools.cache
def theta_tables():
    q = np.arange(T_PARENT)
    first = np.clip((q - 1) // 2 - 2, 0, T_CHILD - 6)
    offset = q * 0.5 - 0.25 - first
    table = np.zeros((T_PARENT, T_CHILD))
    for node in range(6):
        weight = np.ones(T_PARENT)
        for other in range(6):
            if other != node:
                weight = weight * (offset - other) / (node - other)
        table[q, first + node] = weight
    part, pair, place, i = np.meshgrid(np.arange(PARTS), np.arange(32), np.arange(2), np.arange(4), indexing="ij")
    wide, narrow = [], []
    for kid in range(2):
        chip = 2 * pair + (place if kid == 0 else 1 - place)
        rows = table[(12 * chip + 4 * part + i).reshape(-1)]
        rows = rows.reshape(PARTS, 256, T_CHILD)
        wide.append(np.concatenate(split_np(rows), axis=1))
        narrow.append(np.concatenate(split_np(0.25 * rows.transpose(0, 2, 1)), axis=1))
    return np.stack(wide), np.stack(narrow)


@functools.cache
def phi_tables():
    p = np.arange(P_PARENT)[:, None]
    c = np.arange(P_CHILD)[None, :]
    odd = 2 * p - 4 * c - 1
    period = 4 * P_CHILD
    numerator = np.mod((P_CHILD - 1) * odd, 2 * period).astype(np.float64)
    table = np.sin(math.pi * numerator / period) / (P_CHILD * np.sin(math.pi * odd / period))
    plus = np.zeros((4 * LANES, 8 * LANES))
    minus = np.zeros((4 * LANES, 8 * LANES))
    f = np.arange(50)
    for jj in range(4):
        for core in range(2):
            child = 100 * jj + 50 * core + f
            rows = jj * LANES + core * 50 + f
            for dd in range(8):
                parent = 100 * dd + np.arange(100)
                near = table[np.ix_(parent, child)].T
                far = table[np.ix_(parent, child + 400)].T
                at = np.ix_(rows, dd * LANES + np.arange(100))
                plus[at] = 0.5 * (near + far)
                minus[at] = 0.5 * (near - far)
    there = np.stack([np.stack(split_np(plus)), np.stack(split_np(minus))])
    return there, np.ascontiguousarray(there.transpose(0, 1, 3, 2))


@functools.cache
def phi_angles():
    lane = np.arange(16 * LANES)
    phi = 2.0 * math.pi * (100 * (lane // LANES) + lane % LANES + 0.5) / P_PARENT
    return np.stack([np.cos(phi), np.sin(phi)]).reshape(2, 1, 16 * LANES).astype(np.float32)


def split(x):
    high = x.astype(BF16)
    return high, (x - high.astype(F32)).astype(BF16)


def mul(a, b):
    return jnp.dot(a, b, preferred_element_type=F32)


def mul_rows(both, w_high, w_low):
    n = both.shape[0] // 2
    got = mul(both, w_high)
    return got[:n] + got[n:] + mul(both[:n], w_low)


def kernel(
    bas, octant, far_par, far_par_off, far_child, far_child_off, far_count,
    x_hbm, tab_hbm, tabc_hbm, wide_hbm, narrow_hbm, weights_hbm, back_hbm, angles,
    out,
    slot_of, oct_lo, oct_hi, par_src, par_off, kid_src, kid_kid, kid_off, kid_act,
    x_raw, tab_raw, tabc_raw, wide, narrow, weights, weights_back,
    xf, x_swap, x_hi, x_lo, send1, recv1, send2, recv2,
    child_recv, child, tabc, far_out, far_recv, far, tv, tab_send, tab_recv, tab, etab, y, pr, r, acc, own,
    res_recv,
    s_in, s_swap, s_child, s_far, s_tab, s_tabf, s_main, s_back, s_loc,
):
    b = lax.axis_index("box")
    d = lax.axis_index("dir")
    core = lax.rem(d, 2)
    j = d // 2
    me = b * 8 + j
    chip_odd = lax.rem(j, 2) == 1
    buddy = (b, d + 1 - 2 * core)

    def chip(t):
        return (t // 8, lax.rem(t, 8) * 2 + core)

    barrier = pltpu.get_barrier_semaphore()
    pl.semaphore_signal(barrier, inc=1, device_id=buddy, device_id_type=MESH)

    def greet(i, carry):
        pl.semaphore_signal(barrier, inc=1, device_id=chip(lax.rem(me + i, 64)), device_id_type=MESH)
        return carry

    group = jnp.minimum(GROUP * b, 50 - GROUP)
    window = pl.multiple_of((3 * (b // 2)) // 2 * LANES, LANES)
    loads = [
        pltpu.make_async_copy(x_hbm, x_raw, s_in.at[0]),
        pltpu.make_async_copy(wide_hbm, wide, s_in.at[1]),
        pltpu.make_async_copy(tab_hbm.at[:, :, :, pl.ds(window, 256)], tab_raw, s_in.at[2]),
        pltpu.make_async_copy(tabc_hbm.at[pl.ds(group, GROUP)], tabc_raw, s_in.at[3]),
        pltpu.make_async_copy(weights_hbm, weights, s_in.at[4]),
        pltpu.make_async_copy(narrow_hbm, narrow, s_in.at[5]),
        pltpu.make_async_copy(back_hbm, weights_back, s_in.at[6]),
    ]
    loads[0].start()
    lax.fori_loop(1, 64, greet, 0)
    for load in loads[1:]:
        load.start()

    for box in range(8):
        place = jnp.int32(0)
        for s in range(8):
            place = jnp.where(bas[s] == box, s, place)
        slot_of[box] = place
    for s in range(8):
        box = bas[s]
        o0, o1 = octant[2 * box], octant[2 * box + 1]
        oct_lo[s] = jnp.where(chip_odd, o1, o0)
        oct_hi[s] = jnp.where(chip_odd, o0, o1)
        for k in range(FAR_P):
            par_src[s * FAR_P + k] = slot_of[far_par[k, box]]
            par_off[s * FAR_P + k] = far_par_off[k, box]

    def kid_entry(n, carry):
        box = bas[n // 2] * 2 + lax.rem(n, 2)
        for k in range(FAR_C):
            source = far_child[k, box]
            kid_src[n * FAR_C + k] = slot_of[source // 2]
            kid_kid[n * FAR_C + k] = lax.rem(source, 2)
            kid_off[n * FAR_C + k] = far_child_off[k, box]
            kid_act[n * FAR_C + k] = jnp.where(k < far_count[box], 1.0, 0.0).astype(F32)
        return carry

    loads[0].wait()

    def phi_rows(p):
        for c in range(2):
            for k in range(2):
                xf[p, c, k, 0:50, :] = x_raw[:, k, c, p, :]

    for p in range(2):
        pl.when(core != p)(functools.partial(phi_rows, p))

    pl.semaphore_wait(barrier, 64)

    swap = pltpu.make_async_remote_copy(
        src_ref=xf.at[1 - core], dst_ref=x_swap, send_sem=s_swap.at[0], recv_sem=s_swap.at[1],
        device_id=buddy, device_id_type=MESH)
    swap.start()

    def child_start(i, carry):
        g = lax.rem(b + i, 8)
        pltpu.make_async_remote_copy(
            src_ref=x_raw.at[pl.ds(jnp.minimum(GROUP * g, 50 - GROUP), GROUP)], dst_ref=child_recv.at[b],
            send_sem=s_child.at[0], recv_sem=s_child.at[1], device_id=(g, d), device_id_type=MESH).start()
        return carry

    lax.fori_loop(1, 8, child_start, 0)
    child_own = pltpu.make_async_copy(x_raw.at[pl.ds(group, GROUP)], child_recv.at[b], s_loc.at[0])
    child_own.start()

    for p in range(2):
        pl.when(core == p)(functools.partial(phi_rows, p))

    lower = lax.broadcasted_iota(jnp.int32, (8, LANES), 0) < 4
    lane = lax.broadcasted_iota(jnp.int32, (8, LANES), 1)

    y_hi, x_at = j // 4, lax.rem(j, 4)
    other_box = b + 1 - 2 * lax.rem(b, 2)
    first_chip = [b * 8 + y_hi * 4, other_box * 8 + (1 - y_hi) * 4]
    rows = lax.broadcasted_iota(jnp.int32, (96, 256), 0)
    columns = lax.broadcasted_iota(jnp.int32, (96, 256), 1)
    sets = (rows >= 48).astype(jnp.int32)
    parts = (rows >> 4) - 3 * sets
    place = (rows >> 2) & 3
    theta_at = 12 * (jnp.where(rows >= 48, first_chip[1], first_chip[0]) + place) + 4 * parts + (rows & 3) - window
    swapped = theta_at + jnp.where((place & 1) == 0, 12, -12)
    picks = [(columns == q).astype(F32).astype(BF16) for q in (theta_at, swapped)]
    loads[2].wait()
    tv[...] = jnp.zeros_like(tv)

    def tab_prepare(off):
        got = []
        for c in range(2):
            tv[c, 0:100, :] = tab_raw[:, off, c, :]
            high, low = split(jnp.transpose(tv[c]))
            got.append(mul(picks[c], high) + mul(picks[c], low))
        flat = [g.reshape(12, 8, LANES) for g in got]
        even = jnp.where(lower[None], flat[0], flat[1]).reshape(2, 3, 2, 8, LANES)
        odd = jnp.where(lower[None], flat[1], flat[0]).reshape(2, 3, 2, 8, LANES)
        for s in range(2):
            for u in range(2):
                tab_send[s, 2 * u, off] = even[s, :, u]
                tab_send[s, 2 * u + 1, off] = odd[s, :, u]

    def tab_pair(pair, carry):
        tab_prepare(2 * pair)
        tab_prepare(2 * pair + 1)
        at = pl.ds(2 * pair, 2)

        def tab_start(x, carry):
            def go(s):
                box = b if s == 0 else other_box
                half = y_hi if s == 0 else 1 - y_hi
                pltpu.make_async_remote_copy(
                    src_ref=tab_send.at[s, x, at], dst_ref=tab_recv.at[core, j, at],
                    send_sem=s_tab.at[0], recv_sem=s_tab.at[1],
                    device_id=(box, (half * 4 + x) * 2 + core), device_id_type=MESH).start()

            go(1)

            @pl.when(x != x_at)
            def _():
                go(0)

            return carry

        lax.fori_loop(0, 4, tab_start, 0)
        return carry

    lax.fori_loop(0, 4, tab_pair, 0)
    tab_recv[core, j] = tab_send[0, x_at]

    swap.wait()

    def gather_rows(c, carry):
        for k in range(2):
            mine, other = xf[core, c, k, 0:50, :], x_swap[c, k, 0:50, :]
            zero = core == 0
            full = jnp.concatenate(
                [jnp.where(zero, mine, other), jnp.where(zero, other, mine), jnp.zeros((28, T_CHILD), F32)], axis=0)
            high, low = split(jnp.transpose(full))
            x_hi[c, k] = high
            x_lo[c, k] = low
        return carry

    lax.fori_loop(0, 2, gather_rows, 0)
    loads[1].wait()

    def send_all(part, count, send, recv, sems):
        def start(i, carry):
            t = lax.rem(me + i, 64)
            pltpu.make_async_remote_copy(
                src_ref=send.at[part, t, pl.ds(0, count)], dst_ref=recv.at[part, me, pl.ds(0, count)],
                send_sem=sems.at[0, part], recv_sem=sems.at[1, part], device_id=chip(t), device_id_type=MESH).start()
            return carry

        lax.fori_loop(1, 64, start, 0)
        recv[part, me] = send[part, me]

    def wait_all(part, count, ref, sem):
        span = ref.at[part, pl.ds(0, 63), pl.ds(0, count)]
        pltpu.make_async_copy(span, span, sem).wait()

    spare = (lane >= 100) & (lane < 125)

    def stow(m, tile, extra):
        shape = tile.shape
        moved = pltpu.roll(extra.reshape(-1, LANES), 100 - 25 * m, 1).reshape(shape)
        return jnp.where(spare[None], moved, tile)

    def unstow(m, tile, extra):
        shape = tile.shape
        moved = pltpu.roll(tile.reshape(-1, LANES), 28 + 25 * m, 1).reshape(shape)
        return jnp.where(((lane >= 25 * m) & (lane < 25 * m + 25))[None], moved, extra)

    def widen(part, carry):
        for c in range(2):
            got = []
            for k in range(2):
                both = mul(wide[k, part], x_hi[c, k])
                got.append(both[:256] + both[256:] + mul(wide[k, part, 0:256, :], x_lo[c, k]))
            k0 = got[0].reshape(32, 8, LANES)
            k1 = got[1].reshape(32, 8, LANES)
            m = lower[None]
            even = jnp.where(m, k0, k1)
            odd = jnp.where(m, k1, k0)
            both = jnp.stack([even, odd], axis=1).reshape(64, 8, LANES)
            send1[part, :, c * 8:c * 8 + 8, :] = both
        return carry

    lax.fori_loop(0, PARTS, widen, 0)

    def stow_forward(i, carry):
        at = pl.ds(i * 8, 8)
        extra = send1[2, at, 8:16, :]
        for m in range(4):
            half = slice(8 * (m % 2), 8 * (m % 2) + 8)
            send1[m // 2, at, half, :] = stow(m, send1[m // 2, at, half, :], extra)
        return carry

    lax.fori_loop(0, 8, stow_forward, 0)

    def send_forward(part, carry):
        send_all(part, 16, send1, recv1, s_main)
        return carry

    lax.fori_loop(0, 2, send_forward, 0)
    send_all(2, 8, send1, recv1, s_main)

    lax.fori_loop(0, 16, kid_entry, 0)
    loads[3].wait()
    for off in range(16):
        for c in range(2):
            tabc[off, c, 0:GROUP, :] = tabc_raw[:, off, c, :]
    child_own.wait()
    span = child_recv.at[pl.ds(0, 7)]
    pltpu.make_async_copy(span, span, s_child.at[1]).wait()

    def child_rows(src, carry):
        for p in range(2):
            for c in range(2):
                for k in range(2):
                    child[src, p, c, k, 0:GROUP, :] = child_recv[src, :, k, c, p, :]
        return carry

    lax.fori_loop(0, 8, child_rows, 0)

    def far_slot(s, carry):
        for kid in range(2):
            n = s * 2 + kid
            total = [[jnp.zeros((GROUP, T_CHILD), F32) for _ in range(2)] for _ in range(2)]
            for k in range(FAR_C):
                src, sk, off = kid_src[n * FAR_C + k], kid_kid[n * FAR_C + k], kid_off[n * FAR_C + k]
                act = kid_act[n * FAR_C + k]
                tr, ti = tabc[off, 0, 0:GROUP, :] * act, tabc[off, 1, 0:GROUP, :] * act
                for p in range(2):
                    xr, xi = child[src, p, 0, sk, 0:GROUP, :], child[src, p, 1, sk, 0:GROUP, :]
                    total[p][0] = total[p][0] + (tr * xr - ti * xi)
                    total[p][1] = total[p][1] + (tr * xi + ti * xr)
            for p in range(2):
                for c in range(2):
                    far_out[s, 0:GROUP, kid, c, p, :] = total[p][c]
        return carry

    lax.fori_loop(0, 8, far_slot, 0)

    far_row = jnp.where(b == 7, GROUP - 1, 0)

    def far_start(i, carry):
        to = lax.rem(b + i, 8)
        pltpu.make_async_remote_copy(
            src_ref=far_out.at[to, pl.ds(far_row, GROUP)], dst_ref=far_recv.at[b],
            send_sem=s_far.at[0], recv_sem=s_far.at[1], device_id=(to, d), device_id_type=MESH).start()
        return carry

    lax.fori_loop(1, 8, far_start, 0)
    far_own = pltpu.make_async_copy(far_out.at[b, pl.ds(far_row, GROUP)], far_recv.at[b], s_loc.at[1])
    far_own.start()

    span = tab_recv.at[core, pl.ds(0, 7)]
    pltpu.make_async_copy(span, span, s_tab.at[1]).wait()
    tab_on = pltpu.make_async_remote_copy(
        src_ref=tab_recv.at[core], dst_ref=tab_recv.at[core], send_sem=s_tabf.at[0], recv_sem=s_tabf.at[1],
        device_id=buddy, device_id_type=MESH)
    tab_on.start()
    loads[4].wait()
    loads[6].wait()
    tab_on.wait()

    row = lax.broadcasted_iota(jnp.int32, (8, LANES), 0)

    def one_part(part, carry):
        q = (12 * me + 4 * part + lax.rem(row, 4)).astype(F32)
        theta = (q + 0.5) * (math.pi / T_PARENT)
        st, ct = 16.0 * jnp.sin(theta), 16.0 * jnp.cos(theta)

        def prepare(blk, carry):
            at = pl.ds(pl.multiple_of(blk * LANES, LANES), LANES)
            ux, uy = st * angles[0, :, at], st * angles[1, :, at]
            for o in range(4):
                t = ct + (ux if o % 2 else -ux) + (uy if o // 2 else -uy)
                f = t - jnp.round(t)
                a = f * f
                s = f * (3.14159265358979 + a * (-5.16771278004997 + a * (2.55016403987735 + a * (
                    -0.599264529320792 + a * (0.0821458866111282 + a * (-0.00737043094571435
                    + a * 0.000466302805767613))))))
                c = 1.0 + a * (-4.93480220054468 + a * (4.05871212641677 + a * (-1.33526276885459 + a * (
                    0.235330630358893 + a * (-0.0258068913900141 + a * (0.00192957430940392
                    - a * 0.000104638104924846))))))
                cos, sin = 1.0 - 2.0 * (s * s), 2.0 * (s * c)
                etab[4 + o, 0, :, at] = cos
                etab[4 + o, 1, :, at] = sin
                etab[3 - o, 0, :, at] = cos
                etab[3 - o, 1, :, at] = -sin
            dcore, dj = lax.rem(blk, 2), blk // 2
            for off in range(8):
                v = tab_recv[dcore, dj, off, part]
                w = pltpu.roll(v, 4, 0)
                one = jnp.where(lower, v, w)
                two = jnp.where(lower, w, v)
                tab[off, 0, :, at] = jnp.where(chip_odd, two, one)
                tab[off, 1, :, at] = jnp.where(chip_odd, one, two)
            return carry

        lax.fori_loop(0, 16, prepare, 0)

        @pl.when(part < 2)
        def _():
            wait_all(part, 16, recv1, s_main.at[1, part])

        @pl.when(part == 2)
        def _():
            wait_all(2, 8, recv1, s_main.at[1, 2])

            def take(i, carry):
                at = pl.ds(i * 8, 8)
                extra = jnp.zeros((8, 8, LANES), F32)
                for m in range(4):
                    extra = unstow(m, recv1[m // 2, at, 8 * (m % 2):8 * (m % 2) + 8, :], extra)
                recv1[2, at, 8:16, :] = extra
                return carry

            lax.fori_loop(0, 8, take, 0)

        got = recv1[part].reshape(8, 8, 16, LANES)
        for sign in range(2):
            pieces = []
            for jj in range(4):
                one, two = got[:, jj], got[:, jj + 4]
                pieces.append((one + two if sign == 0 else one - two).reshape(128, LANES))
            both = jnp.concatenate(split(jnp.concatenate(pieces, axis=1)), axis=0)
            for n in range(4):
                cols = slice(n * 256, n * 256 + 256)
                wh, wl = weights[sign, 0, :, cols], weights[sign, 1, :, cols]
                y[sign, :, cols] = mul_rows(both, wh, wl)

        def block(dd, carry):
            for half in range(2):
                at_y = pl.ds(pl.multiple_of(dd * LANES, LANES), LANES)
                at = pl.ds(pl.multiple_of((dd + 8 * half) * LANES, LANES), LANES)
                for s in range(8):
                    yp = y[0, s * 16:s * 16 + 16, at_y]
                    ym = y[1, s * 16:s * 16 + 16, at_y]
                    v = yp + ym if half == 0 else yp - ym
                    vr, vi = v[:8], v[8:]
                    cos = jnp.where(lower, etab[oct_lo[s], 0, :, at], etab[oct_hi[s], 0, :, at])
                    sin = jnp.where(lower, etab[oct_lo[s], 1, :, at], etab[oct_hi[s], 1, :, at])
                    re = cos * vr - sin * vi
                    im = sin * vr + cos * vi
                    pr[half, s, 0] = re + pltpu.roll(re, 4, 0)
                    pr[half, s, 1] = im + pltpu.roll(im, 4, 0)
            for s in range(8):
                back = []
                for half in range(2):
                    at = pl.ds(pl.multiple_of((dd + 8 * half) * LANES, LANES), LANES)
                    re = im = None
                    for k in range(FAR_P):
                        src, off = par_src[s * FAR_P + k], par_off[s * FAR_P + k]
                        fr, fi = pr[half, src, 0], pr[half, src, 1]
                        tr, ti = tab[off, 0, :, at], tab[off, 1, :, at]
                        gr, gi = tr * fr - ti * fi, tr * fi + ti * fr
                        re = gr if re is None else re + gr
                        im = gi if im is None else im + gi
                    cos = jnp.where(lower, etab[oct_lo[s], 0, :, at], etab[oct_hi[s], 0, :, at])
                    sin = jnp.where(lower, etab[oct_lo[s], 1, :, at], etab[oct_hi[s], 1, :, at])
                    back.append(jnp.concatenate([cos * re + sin * im, cos * im - sin * re], axis=0))
                at_y = pl.ds(pl.multiple_of(dd * LANES, LANES), LANES)
                for sign in range(2):
                    high, low = split(back[0] + back[1] if sign == 0 else back[0] - back[1])
                    r[sign, s * 16:s * 16 + 16, at_y] = high
                    r[sign, 128 + s * 16:144 + s * 16, at_y] = low
            return carry

        lax.fori_loop(0, 8, block, 0)

        for n in range(2):
            cols = slice(n * 256, n * 256 + 256)
            z = [mul_rows(r[sign], weights_back[sign, 0, :, cols], weights_back[sign, 1, :, cols])
                 for sign in range(2)]
            one, two = z[0] + z[1], z[0] - z[1]
            for h in range(2):
                a = one[:, h * LANES:h * LANES + LANES].reshape(8, 16, LANES)
                c = two[:, h * LANES:h * LANES + LANES].reshape(8, 16, LANES)
                for s in range(8):
                    send2[part, s * 8 + 2 * n + h] = a[s]
                    send2[part, s * 8 + 2 * n + h + 4] = c[s]

        for at_part in range(PARTS):
            @pl.when(part == at_part)
            def _():
                if at_part > 0:
                    def stow_back(i, carry):
                        at = pl.ds(i * 8, 8)
                        extra = send2[0, at, 8:16, :]
                        for h in range(2):
                            half = slice(8 * h, 8 * h + 8)
                            send2[at_part, at, half, :] = stow(
                                2 * at_part - 2 + h, send2[at_part, at, half, :], extra)
                        return carry

                    lax.fori_loop(0, 8, stow_back, 0)
                send_all(at_part, 16 if at_part > 0 else 8, send2, recv2, s_back)

        return carry

    lax.fori_loop(0, PARTS, one_part, 0)

    far_own.wait()
    span = far_recv.at[pl.ds(0, 7)]
    pltpu.make_async_copy(span, span, s_far.at[1]).wait()
    for p in range(2):
        for c in range(2):
            for k in range(2):
                for g in range(8):
                    count = GROUP if g < 7 else 1
                    far[p, c, k, g * GROUP:g * GROUP + count, :] = far_recv[g, 0:count, k, c, p, :]

    loads[5].wait()
    acc[...] = jnp.zeros_like(acc)

    def narrow_tile(part, c):
        got = recv2[part, :, c * 8:c * 8 + 8, :].reshape(32, 2, 8, LANES)
        even, odd = got[:, 0], got[:, 1]
        m = lower[None]
        for k in range(2):
            rows = jnp.where(m, even, odd) if k == 0 else jnp.where(m, odd, even)
            high, low = split(rows.reshape(256, LANES))
            both = mul(narrow[k, part], high)
            acc[c, k] = acc[c, k] + (both[:T_CHILD] + both[T_CHILD:] + mul(narrow[k, part, 0:T_CHILD, :], low))

    wait_all(0, 8, recv2, s_back.at[1, 0])
    narrow_tile(0, 0)

    def narrow_part(part, carry):
        wait_all(part, 16, recv2, s_back.at[1, part])
        for c in range(2):
            narrow_tile(part, c)
        return carry

    lax.fori_loop(1, PARTS, narrow_part, 0)

    def take_back(i, carry):
        at = pl.ds(i * 8, 8)
        extra = jnp.zeros((8, 8, LANES), F32)
        for m in range(4):
            extra = unstow(m, recv2[1 + m // 2, at, 8 * (m % 2):8 * (m % 2) + 8, :], extra)
        recv2[0, at, 8:16, :] = extra
        return carry

    lax.fori_loop(0, 8, take_back, 0)
    narrow_tile(0, 1)

    for c in range(2):
        for k in range(2):
            full = jnp.transpose(acc[c, k])
            own[0, c, k, 0:50, :] = full[0:50]
            own[1, c, k, 0:50, :] = full[50:100]
    swap2 = pltpu.make_async_remote_copy(
        src_ref=own.at[1 - core], dst_ref=res_recv, send_sem=s_swap.at[2], recv_sem=s_swap.at[3],
        device_id=buddy, device_id_type=MESH)
    swap2.start()
    for p in range(2):
        @pl.when(core == p)
        def _():
            for c in range(2):
                for k in range(2):
                    out[:, k, c, p, :] = own[p, c, k, 0:50, :] + far[p, c, k, 0:50, :]

    swap2.wait()
    for p in range(2):
        @pl.when(core != p)
        def _():
            for c in range(2):
                for k in range(2):
                    out[:, k, c, p, :] = res_recv[c, k, 0:50, :] + far[p, c, k, 0:50, :]

    for part in range(PARTS):
        wait_all(part, 8 if part == 2 else 16, send1, s_main.at[0, part])
        wait_all(part, 8 if part == 0 else 16, send2, s_back.at[0, part])
    span = child_recv.at[pl.ds(0, 7)]
    pltpu.make_async_copy(span, span, s_child.at[0]).wait()
    span = far_recv.at[pl.ds(0, 7)]
    pltpu.make_async_copy(span, span, s_far.at[0]).wait()
    span = tab_recv.at[core, pl.ds(0, 7)]
    pltpu.make_async_copy(span, span, s_tab.at[0]).wait()


def shards(child_rad, box_at_slot, octant, far_par, far_par_off, far_child, far_child_off, far_child_count,
           trans_par, trans_child):
    wide, narrow = theta_tables()
    vmem = pl.BlockSpec(memory_space=pltpu.VMEM)
    smem = pl.BlockSpec(memory_space=pltpu.SMEM)
    anywhere = pl.BlockSpec(memory_space=pl.ANY)
    chunks = pltpu.VMEM((PARTS, 64, 16, LANES), F32)
    groups = pltpu.VMEM((8, GROUP, 2, 2, 2, T_CHILD), F32)
    there, back = phi_tables()
    out = pl.pallas_call(
        kernel,
        out_shape=jax.ShapeDtypeStruct((50, 2, 2, 2, T_CHILD), F32),
        in_specs=[smem] * 7 + [anywhere] * 7 + [vmem],
        out_specs=vmem,
        scratch_shapes=[
            pltpu.SMEM((8,), jnp.int32),
            pltpu.SMEM((8,), jnp.int32),
            pltpu.SMEM((8,), jnp.int32),
            pltpu.SMEM((24,), jnp.int32),
            pltpu.SMEM((24,), jnp.int32),
            pltpu.SMEM((112,), jnp.int32),
            pltpu.SMEM((112,), jnp.int32),
            pltpu.SMEM((112,), jnp.int32),
            pltpu.SMEM((112,), F32),
            pltpu.VMEM((50, 2, 2, 2, T_CHILD), F32),
            pltpu.VMEM((100, 8, 2, 256), F32),
            pltpu.VMEM((GROUP, 16, 2, T_CHILD), F32),
            pltpu.VMEM(wide.shape, BF16),
            pltpu.VMEM(narrow.shape, BF16),
            pltpu.VMEM(there.shape, BF16),
            pltpu.VMEM(back.shape, BF16),
            pltpu.VMEM((2, 2, 2, 56, T_CHILD), F32),
            pltpu.VMEM((2, 2, 56, T_CHILD), F32),
            pltpu.VMEM((2, 2, T_CHILD, LANES), BF16),
            pltpu.VMEM((2, 2, T_CHILD, LANES), BF16),
            chunks, chunks, chunks, chunks,
            groups,
            pltpu.VMEM((8, 2, 2, 2, 8, T_CHILD), F32),
            pltpu.VMEM((16, 2, 8, T_CHILD), F32),
            pltpu.VMEM((8, 2 * GROUP - 1, 2, 2, 2, T_CHILD), F32),
            groups,
            pltpu.VMEM((2, 2, 2, 56, T_CHILD), F32),
            pltpu.VMEM((2, LANES, 256), F32),
            pltpu.VMEM((2, 4, 8, PARTS, 8, LANES), F32),
            pltpu.VMEM((2, 8, 8, PARTS, 8, LANES), F32),
            pltpu.VMEM((8, 2, 8, 16 * LANES), F32),
            pltpu.VMEM((8, 2, 8, 16 * LANES), F32),
            pltpu.VMEM((2, 128, 8 * LANES), F32),
            pltpu.VMEM((2, 8, 2, 8, LANES), F32),
            pltpu.VMEM((2, 256, 8 * LANES), BF16),
            pltpu.VMEM((2, 2, T_CHILD, LANES), F32),
            pltpu.VMEM((2, 2, 2, 56, T_CHILD), F32),
            pltpu.VMEM((2, 2, 56, T_CHILD), F32),
            pltpu.SemaphoreType.DMA((7,)),
            pltpu.SemaphoreType.DMA((4,)),
            pltpu.SemaphoreType.DMA((2,)),
            pltpu.SemaphoreType.DMA((2,)),
            pltpu.SemaphoreType.DMA((2,)),
            pltpu.SemaphoreType.DMA((2,)),
            pltpu.SemaphoreType.DMA((2, PARTS)),
            pltpu.SemaphoreType.DMA((2, PARTS)),
            pltpu.SemaphoreType.DMA((2,)),
        ],
        compiler_params=pltpu.CompilerParams(
            collective_id=0, has_side_effects=True, vmem_limit_bytes=60 * 2**20),
        cost_estimate=pl.CostEstimate(flops=14_000_000_000, bytes_accessed=16_000_000, transcendentals=0),
        name="fields",
    )(box_at_slot, octant, far_par.T, far_par_off.T, far_child.T, far_child_off.T, far_child_count,
      child_rad, trans_par, trans_child,
      jnp.asarray(wide), jnp.asarray(narrow), jnp.asarray(there), jnp.asarray(back), jnp.asarray(phi_angles()))
    return out


def solution(mesh):
    return jax.shard_map(
        shards,
        mesh=mesh,
        in_specs=(P("dir", "box", None, None, None), P(), P(), P(), P(), P(), P(), P(),
                  P("dir", None, None, None), P("dir", None, None, None)),
        out_specs=P("dir", "box", None, None, None),
        check_vma=False,
    )
```

```python
import functools
import math

import jax
import jax.numpy as jnp
import numpy as np
from jax import lax
from jax.experimental import pallas as pl
from jax.experimental.pallas import tpu as pltpu
from jax.sharding import PartitionSpec as P

T_CHILD, P_CHILD = 384, 800
T_PARENT, P_PARENT = 768, 1600
FAR_P, FAR_C = 3, 7

PARTS = 3
LANES = 128
GROUP = 7
MESH = pl.DeviceIdType.MESH
F32, BF16 = jnp.float32, jnp.bfloat16


def split_np(table):
    high = table.astype(np.float32).astype(jnp.bfloat16)
    low = (table - high.astype(np.float64)).astype(np.float32).astype(jnp.bfloat16)
    return high, low


@functools.cache
def theta_tables():
    q = np.arange(T_PARENT)
    first = np.clip((q - 1) // 2 - 2, 0, T_CHILD - 6)
    offset = q * 0.5 - 0.25 - first
    table = np.zeros((T_PARENT, T_CHILD))
    for node in range(6):
        weight = np.ones(T_PARENT)
        for other in range(6):
            if other != node:
                weight = weight * (offset - other) / (node - other)
        table[q, first + node] = weight
    part, pair, place, i = np.meshgrid(np.arange(PARTS), np.arange(32), np.arange(2), np.arange(4), indexing="ij")
    wide, narrow = [], []
    for kid in range(2):
        chip = 2 * pair + (place if kid == 0 else 1 - place)
        rows = table[(12 * chip + 4 * part + i).reshape(-1)]
        rows = rows.reshape(PARTS, 256, T_CHILD)
        wide.append(np.concatenate(split_np(rows), axis=1))
        narrow.append(np.concatenate(split_np(0.25 * rows.transpose(0, 2, 1)), axis=1))
    return np.stack(wide), np.stack(narrow)


@functools.cache
def phi_tables():
    p = np.arange(P_PARENT)[:, None]
    c = np.arange(P_CHILD)[None, :]
    odd = 2 * p - 4 * c - 1
    period = 4 * P_CHILD
    numerator = np.mod((P_CHILD - 1) * odd, 2 * period).astype(np.float64)
    table = np.sin(math.pi * numerator / period) / (P_CHILD * np.sin(math.pi * odd / period))
    plus = np.zeros((4 * LANES, 8 * LANES))
    minus = np.zeros((4 * LANES, 8 * LANES))
    f = np.arange(50)
    for jj in range(4):
        for core in range(2):
            child = 100 * jj + 50 * core + f
            rows = jj * LANES + core * 50 + f
            for dd in range(8):
                parent = 100 * dd + np.arange(100)
                near = table[np.ix_(parent, child)].T
                far = table[np.ix_(parent, child + 400)].T
                at = np.ix_(rows, dd * LANES + np.arange(100))
                plus[at] = 0.5 * (near + far)
                minus[at] = 0.5 * (near - far)
    there = np.stack([np.stack(split_np(plus)), np.stack(split_np(minus))])
    return there, np.ascontiguousarray(there.transpose(0, 1, 3, 2))


@functools.cache
def phi_angles():
    lane = np.arange(16 * LANES)
    phi = 2.0 * math.pi * (100 * (lane // LANES) + lane % LANES + 0.5) / P_PARENT
    return np.stack([np.cos(phi), np.sin(phi)]).reshape(2, 1, 16 * LANES).astype(np.float32)


def split(x):
    high = x.astype(BF16)
    return high, (x - high.astype(F32)).astype(BF16)


def mul(a, b):
    return jnp.dot(a, b, preferred_element_type=F32)


def mul_rows(both, w_high, w_low):
    n = both.shape[0] // 2
    got = mul(both, w_high)
    return got[:n] + got[n:] + mul(both[:n], w_low)


def kernel(
    bas, octant, far_par, far_par_off, far_child, far_child_off, far_count,
    x_hbm, tab_hbm, tabc_hbm, wide_hbm, narrow_hbm, weights_hbm, back_hbm, angles,
    out,
    slot_of, oct_lo, oct_hi, par_src, par_off, kid_src, kid_kid, kid_off, kid_act,
    x_raw, tab_raw, tabc_raw, wide, narrow, weights, weights_back,
    xf, x_swap, x_hi, x_lo, send1, recv1, send2, recv2,
    child_recv, child, tabc, far_out, far_recv, far, tv, tab_send, tab_recv, tab, etab, y, pr, r, acc, own,
    res_recv,
    s_in, s_swap, s_child, s_far, s_tab, s_tabf, s_main, s_back, s_loc,
):
    b = lax.axis_index("box")
    d = lax.axis_index("dir")
    core = lax.rem(d, 2)
    j = d // 2
    me = b * 8 + j
    chip_odd = lax.rem(j, 2) == 1
    buddy = (b, d + 1 - 2 * core)

    def chip(t):
        return (t // 8, lax.rem(t, 8) * 2 + core)

    barrier = pltpu.get_barrier_semaphore()
    pl.semaphore_signal(barrier, inc=1, device_id=buddy, device_id_type=MESH)

    def greet(i, carry):
        pl.semaphore_signal(barrier, inc=1, device_id=chip(lax.rem(me + i, 64)), device_id_type=MESH)
        return carry

    group = jnp.minimum(GROUP * b, 50 - GROUP)
    window = pl.multiple_of((3 * (b // 2)) // 2 * LANES, LANES)
    loads = [
        pltpu.make_async_copy(x_hbm, x_raw, s_in.at[0]),
        pltpu.make_async_copy(wide_hbm, wide, s_in.at[1]),
        pltpu.make_async_copy(tab_hbm.at[:, :, :, pl.ds(window, 256)], tab_raw, s_in.at[2]),
        pltpu.make_async_copy(tabc_hbm.at[pl.ds(group, GROUP)], tabc_raw, s_in.at[3]),
        pltpu.make_async_copy(weights_hbm, weights, s_in.at[4]),
        pltpu.make_async_copy(narrow_hbm, narrow, s_in.at[5]),
        pltpu.make_async_copy(back_hbm, weights_back, s_in.at[6]),
    ]
    loads[0].start()
    lax.fori_loop(1, 64, greet, 0)
    for load in loads[1:]:
        load.start()

    for box in range(8):
        place = jnp.int32(0)
        for s in range(8):
            place = jnp.where(bas[s] == box, s, place)
        slot_of[box] = place
    for s in range(8):
        box = bas[s]
        o0, o1 = octant[2 * box], octant[2 * box + 1]
        oct_lo[s] = jnp.where(chip_odd, o1, o0)
        oct_hi[s] = jnp.where(chip_odd, o0, o1)
        for k in range(FAR_P):
            par_src[s * FAR_P + k] = slot_of[far_par[k, box]]
            par_off[s * FAR_P + k] = far_par_off[k, box]

    def kid_entry(n, carry):
        box = bas[n // 2] * 2 + lax.rem(n, 2)
        for k in range(FAR_C):
            source = far_child[k, box]
            kid_src[n * FAR_C + k] = slot_of[source // 2]
            kid_kid[n * FAR_C + k] = lax.rem(source, 2)
            kid_off[n * FAR_C + k] = far_child_off[k, box]
            kid_act[n * FAR_C + k] = jnp.where(k < far_count[box], 1.0, 0.0).astype(F32)
        return carry

    loads[0].wait()

    def phi_rows(p):
        for c in range(2):
            for k in range(2):
                xf[p, c, k, 0:50, :] = x_raw[:, k, c, p, :]

    for p in range(2):
        pl.when(core != p)(functools.partial(phi_rows, p))

    pl.semaphore_wait(barrier, 64)

    swap = pltpu.make_async_remote_copy(
        src_ref=xf.at[1 - core], dst_ref=x_swap, send_sem=s_swap.at[0], recv_sem=s_swap.at[1],
        device_id=buddy, device_id_type=MESH)
    swap.start()

    def child_start(i, carry):
        g = lax.rem(b + i, 8)
        pltpu.make_async_remote_copy(
            src_ref=x_raw.at[pl.ds(jnp.minimum(GROUP * g, 50 - GROUP), GROUP)], dst_ref=child_recv.at[b],
            send_sem=s_child.at[0], recv_sem=s_child.at[1], device_id=(g, d), device_id_type=MESH).start()
        return carry

    lax.fori_loop(1, 8, child_start, 0)
    child_own = pltpu.make_async_copy(x_raw.at[pl.ds(group, GROUP)], child_recv.at[b], s_loc.at[0])
    child_own.start()

    for p in range(2):
        pl.when(core == p)(functools.partial(phi_rows, p))

    lower = lax.broadcasted_iota(jnp.int32, (8, LANES), 0) < 4
    lane = lax.broadcasted_iota(jnp.int32, (8, LANES), 1)

    y_hi, x_at = j // 4, lax.rem(j, 4)
    other_box = b + 1 - 2 * lax.rem(b, 2)
    first_chip = [b * 8 + y_hi * 4, other_box * 8 + (1 - y_hi) * 4]
    rows = lax.broadcasted_iota(jnp.int32, (96, 256), 0)
    columns = lax.broadcasted_iota(jnp.int32, (96, 256), 1)
    sets = (rows >= 48).astype(jnp.int32)
    parts = (rows >> 4) - 3 * sets
    place = (rows >> 2) & 3
    theta_at = 12 * (jnp.where(rows >= 48, first_chip[1], first_chip[0]) + place) + 4 * parts + (rows & 3) - window
    swapped = theta_at + jnp.where((place & 1) == 0, 12, -12)
    picks = [(columns == q).astype(F32).astype(BF16) for q in (theta_at, swapped)]
    loads[2].wait()
    tv[...] = jnp.zeros_like(tv)

    def tab_prepare(off):
        got = []
        for c in range(2):
            tv[c, 0:100, :] = tab_raw[:, off, c, :]
            high, low = split(jnp.transpose(tv[c]))
            got.append(mul(picks[c], high) + mul(picks[c], low))
        flat = [g.reshape(12, 8, LANES) for g in got]
        even = jnp.where(lower[None], flat[0], flat[1]).reshape(2, 3, 2, 8, LANES)
        odd = jnp.where(lower[None], flat[1], flat[0]).reshape(2, 3, 2, 8, LANES)
        for s in range(2):
            for u in range(2):
                tab_send[s, 2 * u, off] = even[s, :, u]
                tab_send[s, 2 * u + 1, off] = odd[s, :, u]

    def tab_pair(pair, carry):
        tab_prepare(2 * pair)
        tab_prepare(2 * pair + 1)
        at = pl.ds(2 * pair, 2)

        def tab_start(x, carry):
            def go(s):
                box = b if s == 0 else other_box
                half = y_hi if s == 0 else 1 - y_hi
                pltpu.make_async_remote_copy(
                    src_ref=tab_send.at[s, x, at], dst_ref=tab_recv.at[core, j, at],
                    send_sem=s_tab.at[0], recv_sem=s_tab.at[1],
                    device_id=(box, (half * 4 + x) * 2 + core), device_id_type=MESH).start()

            go(1)

            @pl.when(x != x_at)
            def _():
                go(0)

            return carry

        lax.fori_loop(0, 4, tab_start, 0)
        return carry

    lax.fori_loop(0, 4, tab_pair, 0)
    tab_recv[core, j] = tab_send[0, x_at]

    swap.wait()

    def gather_rows(c, carry):
        for k in range(2):
            mine, other = xf[core, c, k, 0:50, :], x_swap[c, k, 0:50, :]
            zero = core == 0
            full = jnp.concatenate(
                [jnp.where(zero, mine, other), jnp.where(zero, other, mine), jnp.zeros((28, T_CHILD), F32)], axis=0)
            high, low = split(jnp.transpose(full))
            x_hi[c, k] = high
            x_lo[c, k] = low
        return carry

    lax.fori_loop(0, 2, gather_rows, 0)
    loads[1].wait()

    def send_all(part, count, send, recv, sems):
        def start(i, carry):
            t = lax.rem(me + i, 64)
            pltpu.make_async_remote_copy(
                src_ref=send.at[part, t, pl.ds(0, count)], dst_ref=recv.at[part, me, pl.ds(0, count)],
                send_sem=sems.at[0, part], recv_sem=sems.at[1, part], device_id=chip(t), device_id_type=MESH).start()
            return carry

        lax.fori_loop(1, 64, start, 0)
        recv[part, me] = send[part, me]

    def wait_all(part, count, ref, sem):
        span = ref.at[part, pl.ds(0, 63), pl.ds(0, count)]
        pltpu.make_async_copy(span, span, sem).wait()

    spare = (lane >= 100) & (lane < 125)

    def stow(m, tile, extra):
        shape = tile.shape
        moved = pltpu.roll(extra.reshape(-1, LANES), 100 - 25 * m, 1).reshape(shape)
        return jnp.where(spare[None], moved, tile)

    def unstow(m, tile, extra):
        shape = tile.shape
        moved = pltpu.roll(tile.reshape(-1, LANES), 28 + 25 * m, 1).reshape(shape)
        return jnp.where(((lane >= 25 * m) & (lane < 25 * m + 25))[None], moved, extra)

    def widen(part, carry):
        for c in range(2):
            got = []
            for k in range(2):
                both = mul(wide[k, part], x_hi[c, k])
                got.append(both[:256] + both[256:] + mul(wide[k, part, 0:256, :], x_lo[c, k]))
            k0 = got[0].reshape(32, 8, LANES)
            k1 = got[1].reshape(32, 8, LANES)
            m = lower[None]
            even = jnp.where(m, k0, k1)
            odd = jnp.where(m, k1, k0)
            both = jnp.stack([even, odd], axis=1).reshape(64, 8, LANES)
            send1[part, :, c * 8:c * 8 + 8, :] = both
        return carry

    lax.fori_loop(0, PARTS, widen, 0)

    def stow_forward(i, carry):
        at = pl.ds(i * 8, 8)
        extra = send1[2, at, 8:16, :]
        for m in range(4):
            half = slice(8 * (m % 2), 8 * (m % 2) + 8)
            send1[m // 2, at, half, :] = stow(m, send1[m // 2, at, half, :], extra)
        return carry

    lax.fori_loop(0, 8, stow_forward, 0)

    def send_forward(part, carry):
        send_all(part, 16, send1, recv1, s_main)
        return carry

    lax.fori_loop(0, 2, send_forward, 0)
    send_all(2, 8, send1, recv1, s_main)

    lax.fori_loop(0, 16, kid_entry, 0)
    loads[3].wait()
    for off in range(16):
        for c in range(2):
            tabc[off, c, 0:GROUP, :] = tabc_raw[:, off, c, :]
    child_own.wait()
    span = child_recv.at[pl.ds(0, 7)]
    pltpu.make_async_copy(span, span, s_child.at[1]).wait()

    def child_rows(src, carry):
        for p in range(2):
            for c in range(2):
                for k in range(2):
                    child[src, p, c, k, 0:GROUP, :] = child_recv[src, :, k, c, p, :]
        return carry

    lax.fori_loop(0, 8, child_rows, 0)

    def far_slot(s, carry):
        for kid in range(2):
            n = s * 2 + kid
            total = [[jnp.zeros((GROUP, T_CHILD), F32) for _ in range(2)] for _ in range(2)]
            for k in range(FAR_C):
                src, sk, off = kid_src[n * FAR_C + k], kid_kid[n * FAR_C + k], kid_off[n * FAR_C + k]
                act = kid_act[n * FAR_C + k]
                tr, ti = tabc[off, 0, 0:GROUP, :] * act, tabc[off, 1, 0:GROUP, :] * act
                for p in range(2):
                    xr, xi = child[src, p, 0, sk, 0:GROUP, :], child[src, p, 1, sk, 0:GROUP, :]
                    total[p][0] = total[p][0] + (tr * xr - ti * xi)
                    total[p][1] = total[p][1] + (tr * xi + ti * xr)
            for p in range(2):
                for c in range(2):
                    far_out[s, 0:GROUP, kid, c, p, :] = total[p][c]
        return carry

    lax.fori_loop(0, 8, far_slot, 0)

    far_row = jnp.where(b == 7, GROUP - 1, 0)

    def far_start(i, carry):
        to = lax.rem(b + i, 8)
        pltpu.make_async_remote_copy(
            src_ref=far_out.at[to, pl.ds(far_row, GROUP)], dst_ref=far_recv.at[b],
            send_sem=s_far.at[0], recv_sem=s_far.at[1], device_id=(to, d), device_id_type=MESH).start()
        return carry

    lax.fori_loop(1, 8, far_start, 0)
    far_own = pltpu.make_async_copy(far_out.at[b, pl.ds(far_row, GROUP)], far_recv.at[b], s_loc.at[1])
    far_own.start()

    row = lax.broadcasted_iota(jnp.int32, (8, LANES), 0)

    def shift_tables(part, carry):
        q = (12 * me + 4 * part + lax.rem(row, 4)).astype(F32)
        theta = (q + 0.5) * (math.pi / T_PARENT)
        st, ct = 16.0 * jnp.sin(theta), 16.0 * jnp.cos(theta)

        def shifts(blk, carry):
            at = pl.ds(pl.multiple_of(blk * LANES, LANES), LANES)
            ux, uy = st * angles[0, :, at], st * angles[1, :, at]
            for o in range(4):
                t = ct + (ux if o % 2 else -ux) + (uy if o // 2 else -uy)
                f = t - jnp.round(t)
                a = f * f
                s = f * (3.14159265358979 + a * (-5.16771278004997 + a * (2.55016403987735 + a * (
                    -0.599264529320792 + a * (0.0821458866111282 + a * (-0.00737043094571435
                    + a * 0.000466302805767613))))))
                c = 1.0 + a * (-4.93480220054468 + a * (4.05871212641677 + a * (-1.33526276885459 + a * (
                    0.235330630358893 + a * (-0.0258068913900141 + a * (0.00192957430940392
                    - a * 0.000104638104924846))))))
                cos, sin = 1.0 - 2.0 * (s * s), 2.0 * (s * c)
                etab[part, 4 + o, 0, :, at] = cos
                etab[part, 4 + o, 1, :, at] = sin
                etab[part, 3 - o, 0, :, at] = cos
                etab[part, 3 - o, 1, :, at] = -sin
            return carry

        lax.fori_loop(0, 16, shifts, 0)
        return carry

    lax.fori_loop(0, PARTS, shift_tables, 0)

    span = tab_recv.at[core, pl.ds(0, 7)]
    pltpu.make_async_copy(span, span, s_tab.at[1]).wait()
    tab_on = pltpu.make_async_remote_copy(
        src_ref=tab_recv.at[core], dst_ref=tab_recv.at[core], send_sem=s_tabf.at[0], recv_sem=s_tabf.at[1],
        device_id=buddy, device_id_type=MESH)
    tab_on.start()
    loads[4].wait()
    loads[6].wait()
    tab_on.wait()

    def one_part(part, carry):
        def prepare(blk, carry):
            at = pl.ds(pl.multiple_of(blk * LANES, LANES), LANES)
            dcore, dj = lax.rem(blk, 2), blk // 2
            for off in range(8):
                v = tab_recv[dcore, dj, off, part]
                w = pltpu.roll(v, 4, 0)
                one = jnp.where(lower, v, w)
                two = jnp.where(lower, w, v)
                tab[off, 0, :, at] = jnp.where(chip_odd, two, one)
                tab[off, 1, :, at] = jnp.where(chip_odd, one, two)
            return carry

        lax.fori_loop(0, 16, prepare, 0)

        @pl.when(part < 2)
        def _():
            wait_all(part, 16, recv1, s_main.at[1, part])

        @pl.when(part == 2)
        def _():
            wait_all(2, 8, recv1, s_main.at[1, 2])

            def take(i, carry):
                at = pl.ds(i * 8, 8)
                extra = jnp.zeros((8, 8, LANES), F32)
                for m in range(4):
                    extra = unstow(m, recv1[m // 2, at, 8 * (m % 2):8 * (m % 2) + 8, :], extra)
                recv1[2, at, 8:16, :] = extra
                return carry

            lax.fori_loop(0, 8, take, 0)

        got = recv1[part].reshape(8, 8, 16, LANES)
        for sign in range(2):
            pieces = []
            for jj in range(4):
                one, two = got[:, jj], got[:, jj + 4]
                pieces.append((one + two if sign == 0 else one - two).reshape(128, LANES))
            both = jnp.concatenate(split(jnp.concatenate(pieces, axis=1)), axis=0)
            for n in range(4):
                cols = slice(n * 256, n * 256 + 256)
                wh, wl = weights[sign, 0, :, cols], weights[sign, 1, :, cols]
                y[sign, :, cols] = mul_rows(both, wh, wl)

        def block(dd, carry):
            for half in range(2):
                at_y = pl.ds(pl.multiple_of(dd * LANES, LANES), LANES)
                at = pl.ds(pl.multiple_of((dd + 8 * half) * LANES, LANES), LANES)
                for s in range(8):
                    yp = y[0, s * 16:s * 16 + 16, at_y]
                    ym = y[1, s * 16:s * 16 + 16, at_y]
                    v = yp + ym if half == 0 else yp - ym
                    vr, vi = v[:8], v[8:]
                    cos = jnp.where(lower, etab[part, oct_lo[s], 0, :, at], etab[part, oct_hi[s], 0, :, at])
                    sin = jnp.where(lower, etab[part, oct_lo[s], 1, :, at], etab[part, oct_hi[s], 1, :, at])
                    re = cos * vr - sin * vi
                    im = sin * vr + cos * vi
                    pr[half, s, 0] = re + pltpu.roll(re, 4, 0)
                    pr[half, s, 1] = im + pltpu.roll(im, 4, 0)
            for s in range(8):
                back = []
                for half in range(2):
                    at = pl.ds(pl.multiple_of((dd + 8 * half) * LANES, LANES), LANES)
                    re = im = None
                    for k in range(FAR_P):
                        src, off = par_src[s * FAR_P + k], par_off[s * FAR_P + k]
                        fr, fi = pr[half, src, 0], pr[half, src, 1]
                        tr, ti = tab[off, 0, :, at], tab[off, 1, :, at]
                        gr, gi = tr * fr - ti * fi, tr * fi + ti * fr
                        re = gr if re is None else re + gr
                        im = gi if im is None else im + gi
                    cos = jnp.where(lower, etab[part, oct_lo[s], 0, :, at], etab[part, oct_hi[s], 0, :, at])
                    sin = jnp.where(lower, etab[part, oct_lo[s], 1, :, at], etab[part, oct_hi[s], 1, :, at])
                    back.append(jnp.concatenate([cos * re + sin * im, cos * im - sin * re], axis=0))
                at_y = pl.ds(pl.multiple_of(dd * LANES, LANES), LANES)
                for sign in range(2):
                    high, low = split(back[0] + back[1] if sign == 0 else back[0] - back[1])
                    r[sign, s * 16:s * 16 + 16, at_y] = high
                    r[sign, 128 + s * 16:144 + s * 16, at_y] = low
            return carry

        lax.fori_loop(0, 8, block, 0)

        for n in range(2):
            cols = slice(n * 256, n * 256 + 256)
            z = [mul_rows(r[sign], weights_back[sign, 0, :, cols], weights_back[sign, 1, :, cols])
                 for sign in range(2)]
            one, two = z[0] + z[1], z[0] - z[1]
            for h in range(2):
                a = one[:, h * LANES:h * LANES + LANES].reshape(8, 16, LANES)
                c = two[:, h * LANES:h * LANES + LANES].reshape(8, 16, LANES)
                for s in range(8):
                    send2[part, s * 8 + 2 * n + h] = a[s]
                    send2[part, s * 8 + 2 * n + h + 4] = c[s]

        for at_part in range(PARTS):
            @pl.when(part == at_part)
            def _():
                if at_part > 0:
                    def stow_back(i, carry):
                        at = pl.ds(i * 8, 8)
                        extra = send2[0, at, 8:16, :]
                        for h in range(2):
                            half = slice(8 * h, 8 * h + 8)
                            send2[at_part, at, half, :] = stow(
                                2 * at_part - 2 + h, send2[at_part, at, half, :], extra)
                        return carry

                    lax.fori_loop(0, 8, stow_back, 0)
                send_all(at_part, 16 if at_part > 0 else 8, send2, recv2, s_back)

        return carry

    lax.fori_loop(0, PARTS, one_part, 0)

    far_own.wait()
    span = far_recv.at[pl.ds(0, 7)]
    pltpu.make_async_copy(span, span, s_far.at[1]).wait()
    for p in range(2):
        for c in range(2):
            for k in range(2):
                for g in range(8):
                    count = GROUP if g < 7 else 1
                    far[p, c, k, g * GROUP:g * GROUP + count, :] = far_recv[g, 0:count, k, c, p, :]

    loads[5].wait()
    acc[...] = jnp.zeros_like(acc)

    def narrow_tile(part, c):
        got = recv2[part, :, c * 8:c * 8 + 8, :].reshape(32, 2, 8, LANES)
        even, odd = got[:, 0], got[:, 1]
        m = lower[None]
        for k in range(2):
            rows = jnp.where(m, even, odd) if k == 0 else jnp.where(m, odd, even)
            high, low = split(rows.reshape(256, LANES))
            both = mul(narrow[k, part], high)
            acc[c, k] = acc[c, k] + (both[:T_CHILD] + both[T_CHILD:] + mul(narrow[k, part, 0:T_CHILD, :], low))

    wait_all(0, 8, recv2, s_back.at[1, 0])
    narrow_tile(0, 0)

    def hand_over(c):
        return pltpu.make_async_remote_copy(
            src_ref=own.at[1 - core, c], dst_ref=res_recv.at[c], send_sem=s_swap.at[2 + c], recv_sem=s_swap.at[4 + c],
            device_id=buddy, device_id_type=MESH)

    def finish(c):
        for k in range(2):
            full = jnp.transpose(acc[c, k])
            own[0, c, k, 0:50, :] = full[0:50]
            own[1, c, k, 0:50, :] = full[50:100]
        hand_over(c).start()

    def keep(c):
        for p in range(2):
            @pl.when(core == p)
            def _():
                for k in range(2):
                    out[:, k, c, p, :] = own[p, c, k, 0:50, :] + far[p, c, k, 0:50, :]

    def take_over(c):
        hand_over(c).wait()
        for p in range(2):
            @pl.when(core != p)
            def _():
                for k in range(2):
                    out[:, k, c, p, :] = res_recv[c, k, 0:50, :] + far[p, c, k, 0:50, :]

    wait_all(1, 16, recv2, s_back.at[1, 1])
    narrow_tile(1, 0)
    narrow_tile(1, 1)
    wait_all(2, 16, recv2, s_back.at[1, 2])
    narrow_tile(2, 0)
    finish(0)

    def take_back(i, carry):
        at = pl.ds(i * 8, 8)
        extra = jnp.zeros((8, 8, LANES), F32)
        for m in range(4):
            extra = unstow(m, recv2[1 + m // 2, at, 8 * (m % 2):8 * (m % 2) + 8, :], extra)
        recv2[0, at, 8:16, :] = extra
        return carry

    lax.fori_loop(0, 8, take_back, 0)
    narrow_tile(2, 1)
    narrow_tile(0, 1)
    finish(1)
    keep(0)
    keep(1)
    take_over(0)
    take_over(1)

    for part in range(PARTS):
        wait_all(part, 8 if part == 2 else 16, send1, s_main.at[0, part])
        wait_all(part, 8 if part == 0 else 16, send2, s_back.at[0, part])
    span = child_recv.at[pl.ds(0, 7)]
    pltpu.make_async_copy(span, span, s_child.at[0]).wait()
    span = far_recv.at[pl.ds(0, 7)]
    pltpu.make_async_copy(span, span, s_far.at[0]).wait()
    span = tab_recv.at[core, pl.ds(0, 7)]
    pltpu.make_async_copy(span, span, s_tab.at[0]).wait()


def shards(child_rad, box_at_slot, octant, far_par, far_par_off, far_child, far_child_off, far_child_count,
           trans_par, trans_child):
    wide, narrow = theta_tables()
    vmem = pl.BlockSpec(memory_space=pltpu.VMEM)
    smem = pl.BlockSpec(memory_space=pltpu.SMEM)
    anywhere = pl.BlockSpec(memory_space=pl.ANY)
    chunks = pltpu.VMEM((PARTS, 64, 16, LANES), F32)
    groups = pltpu.VMEM((8, GROUP, 2, 2, 2, T_CHILD), F32)
    there, back = phi_tables()
    out = pl.pallas_call(
        kernel,
        out_shape=pltpu.VMEM((50, 2, 2, 2, T_CHILD), F32),
        in_specs=[smem] * 7 + [anywhere] * 7 + [vmem],
        out_specs=vmem,
        scratch_shapes=[
            pltpu.SMEM((8,), jnp.int32),
            pltpu.SMEM((8,), jnp.int32),
            pltpu.SMEM((8,), jnp.int32),
            pltpu.SMEM((24,), jnp.int32),
            pltpu.SMEM((24,), jnp.int32),
            pltpu.SMEM((112,), jnp.int32),
            pltpu.SMEM((112,), jnp.int32),
            pltpu.SMEM((112,), jnp.int32),
            pltpu.SMEM((112,), F32),
            pltpu.VMEM((50, 2, 2, 2, T_CHILD), F32),
            pltpu.VMEM((100, 8, 2, 256), F32),
            pltpu.VMEM((GROUP, 16, 2, T_CHILD), F32),
            pltpu.VMEM(wide.shape, BF16),
            pltpu.VMEM(narrow.shape, BF16),
            pltpu.VMEM(there.shape, BF16),
            pltpu.VMEM(back.shape, BF16),
            pltpu.VMEM((2, 2, 2, 56, T_CHILD), F32),
            pltpu.VMEM((2, 2, 56, T_CHILD), F32),
            pltpu.VMEM((2, 2, T_CHILD, LANES), BF16),
            pltpu.VMEM((2, 2, T_CHILD, LANES), BF16),
            chunks, chunks, chunks, chunks,
            groups,
            pltpu.VMEM((8, 2, 2, 2, 8, T_CHILD), F32),
            pltpu.VMEM((16, 2, 8, T_CHILD), F32),
            pltpu.VMEM((8, 2 * GROUP - 1, 2, 2, 2, T_CHILD), F32),
            groups,
            pltpu.VMEM((2, 2, 2, 56, T_CHILD), F32),
            pltpu.VMEM((2, LANES, 256), F32),
            pltpu.VMEM((2, 4, 8, PARTS, 8, LANES), F32),
            pltpu.VMEM((2, 8, 8, PARTS, 8, LANES), F32),
            pltpu.VMEM((8, 2, 8, 16 * LANES), F32),
            pltpu.VMEM((PARTS, 8, 2, 8, 16 * LANES), F32),
            pltpu.VMEM((2, 128, 8 * LANES), F32),
            pltpu.VMEM((2, 8, 2, 8, LANES), F32),
            pltpu.VMEM((2, 256, 8 * LANES), BF16),
            pltpu.VMEM((2, 2, T_CHILD, LANES), F32),
            pltpu.VMEM((2, 2, 2, 56, T_CHILD), F32),
            pltpu.VMEM((2, 2, 56, T_CHILD), F32),
            pltpu.SemaphoreType.DMA((7,)),
            pltpu.SemaphoreType.DMA((6,)),
            pltpu.SemaphoreType.DMA((2,)),
            pltpu.SemaphoreType.DMA((2,)),
            pltpu.SemaphoreType.DMA((2,)),
            pltpu.SemaphoreType.DMA((2,)),
            pltpu.SemaphoreType.DMA((2, PARTS)),
            pltpu.SemaphoreType.DMA((2, PARTS)),
            pltpu.SemaphoreType.DMA((2,)),
        ],
        compiler_params=pltpu.CompilerParams(
            collective_id=0, has_side_effects=True, vmem_limit_bytes=60 * 2**20),
        cost_estimate=pl.CostEstimate(flops=14_000_000_000, bytes_accessed=16_000_000, transcendentals=0),
        name="fields",
    )(box_at_slot, octant, far_par.T, far_par_off.T, far_child.T, far_child_off.T, far_child_count,
      child_rad, trans_par, trans_child,
      jnp.asarray(wide), jnp.asarray(narrow), jnp.asarray(there), jnp.asarray(back), jnp.asarray(phi_angles()))
    return out


def solution(mesh):
    return jax.shard_map(
        shards,
        mesh=mesh,
        in_specs=(P("dir", "box", None, None, None), P(), P(), P(), P(), P(), P(), P(),
                  P("dir", None, None, None), P("dir", None, None, None)),
        out_specs=P("dir", "box", None, None, None),
        check_vma=False,
    )
```

```python
import functools
import math

import jax
import jax.numpy as jnp
import numpy as np
from jax import lax
from jax.experimental import pallas as pl
from jax.experimental.pallas import tpu as pltpu
from jax.sharding import PartitionSpec as P

T_CHILD, P_CHILD = 384, 800
T_PARENT, P_PARENT = 768, 1600
FAR_P, FAR_C = 3, 7

PARTS = 3
LANES = 128
GROUP = 7
MESH = pl.DeviceIdType.MESH
F32, BF16 = jnp.float32, jnp.bfloat16


def split_np(table):
    high = table.astype(np.float32).astype(jnp.bfloat16)
    low = (table - high.astype(np.float64)).astype(np.float32).astype(jnp.bfloat16)
    return high, low


@functools.cache
def theta_tables():
    q = np.arange(T_PARENT)
    first = np.clip((q - 1) // 2 - 2, 0, T_CHILD - 6)
    offset = q * 0.5 - 0.25 - first
    table = np.zeros((T_PARENT, T_CHILD))
    for node in range(6):
        weight = np.ones(T_PARENT)
        for other in range(6):
            if other != node:
                weight = weight * (offset - other) / (node - other)
        table[q, first + node] = weight
    part, pair, place, i = np.meshgrid(np.arange(PARTS), np.arange(32), np.arange(2), np.arange(4), indexing="ij")
    wide, narrow = [], []
    for kid in range(2):
        chip = 2 * pair + (place if kid == 0 else 1 - place)
        rows = table[(12 * chip + 4 * part + i).reshape(-1)]
        rows = rows.reshape(PARTS, 256, T_CHILD)
        wide.append(np.concatenate(split_np(rows), axis=1))
        narrow.append(np.concatenate(split_np(0.25 * rows.transpose(0, 2, 1)), axis=1))
    return np.stack(wide), np.stack(narrow)


@functools.cache
def phi_tables():
    p = np.arange(P_PARENT)[:, None]
    c = np.arange(P_CHILD)[None, :]
    odd = 2 * p - 4 * c - 1
    period = 4 * P_CHILD
    numerator = np.mod((P_CHILD - 1) * odd, 2 * period).astype(np.float64)
    table = np.sin(math.pi * numerator / period) / (P_CHILD * np.sin(math.pi * odd / period))
    plus = np.zeros((4 * LANES, 8 * LANES))
    minus = np.zeros((4 * LANES, 8 * LANES))
    f = np.arange(50)
    for jj in range(4):
        for core in range(2):
            child = 100 * jj + 50 * core + f
            rows = jj * LANES + core * 50 + f
            for dd in range(8):
                parent = 100 * dd + np.arange(100)
                near = table[np.ix_(parent, child)].T
                far = table[np.ix_(parent, child + 400)].T
                at = np.ix_(rows, dd * LANES + np.arange(100))
                plus[at] = 0.5 * (near + far)
                minus[at] = 0.5 * (near - far)
    there = np.stack([np.stack(split_np(plus)), np.stack(split_np(minus))])
    return there, np.ascontiguousarray(there.transpose(0, 1, 3, 2))


@functools.cache
def phi_angles():
    lane = np.arange(16 * LANES)
    phi = 2.0 * math.pi * (100 * (lane // LANES) + lane % LANES + 0.5) / P_PARENT
    return np.stack([np.cos(phi), np.sin(phi)]).reshape(2, 1, 16 * LANES).astype(np.float32)


def split(x):
    high = x.astype(BF16)
    return high, (x - high.astype(F32)).astype(BF16)


def mul(a, b):
    return jnp.dot(a, b, preferred_element_type=F32)


def mul_rows(both, w_high, w_low):
    n = both.shape[0] // 2
    got = mul(both, w_high)
    return got[:n] + got[n:] + mul(both[:n], w_low)


def kernel(
    bas, octant, far_par, far_par_off, far_child, far_child_off, far_count,
    x_hbm, tab_hbm, tabc_hbm, wide_hbm, narrow_hbm, weights_hbm, back_hbm, angles,
    out,
    slot_of, oct_lo, oct_hi, par_src, par_off, kid_src, kid_kid, kid_off, kid_act,
    x_raw, tab_raw, tabc_raw, wide, narrow, weights, weights_back,
    xf, x_swap, x_hi, x_lo, send1, recv1, send2, recv2,
    child_recv, child, tabc, far_out, far_recv, far, tv, tab_send, tab_recv, tab, etab, y, pr, r, acc, own,
    res_recv,
    s_in, s_swap, s_child, s_far, s_tab, s_tabf, s_main, s_back, s_loc,
):
    b = lax.axis_index("box")
    d = lax.axis_index("dir")
    core = lax.rem(d, 2)
    j = d // 2
    me = b * 8 + j
    chip_odd = lax.rem(j, 2) == 1
    buddy = (b, d + 1 - 2 * core)

    def chip(t):
        return (t // 8, lax.rem(t, 8) * 2 + core)

    barrier = pltpu.get_barrier_semaphore()
    pl.semaphore_signal(barrier, inc=1, device_id=buddy, device_id_type=MESH)

    def greet(i, carry):
        pl.semaphore_signal(barrier, inc=1, device_id=chip(lax.rem(me + i, 64)), device_id_type=MESH)
        return carry

    def group_of(g):
        return 6 * g + jnp.maximum(g - 6, 0)

    group = group_of(b)
    window = pl.multiple_of((3 * (b // 2)) // 2 * LANES, LANES)
    loads = [
        pltpu.make_async_copy(x_hbm, x_raw, s_in.at[0]),
        pltpu.make_async_copy(wide_hbm, wide, s_in.at[1]),
        pltpu.make_async_copy(tab_hbm.at[:, :, :, pl.ds(window, 256)], tab_raw, s_in.at[2]),
        pltpu.make_async_copy(tabc_hbm.at[pl.ds(group, GROUP)], tabc_raw, s_in.at[3]),
        pltpu.make_async_copy(weights_hbm, weights, s_in.at[4]),
        pltpu.make_async_copy(narrow_hbm, narrow, s_in.at[5]),
        pltpu.make_async_copy(back_hbm, weights_back, s_in.at[6]),
    ]
    loads[0].start()
    lax.fori_loop(1, 64, greet, 0)
    for load in loads[1:]:
        load.start()

    for box in range(8):
        place = jnp.int32(0)
        for s in range(8):
            place = jnp.where(bas[s] == box, s, place)
        slot_of[box] = place
    for s in range(8):
        box = bas[s]
        o0, o1 = octant[2 * box], octant[2 * box + 1]
        oct_lo[s] = jnp.where(chip_odd, o1, o0)
        oct_hi[s] = jnp.where(chip_odd, o0, o1)
        for k in range(FAR_P):
            par_src[s * FAR_P + k] = slot_of[far_par[k, box]]
            par_off[s * FAR_P + k] = far_par_off[k, box]

    def kid_entry(n, carry):
        box = bas[n // 2] * 2 + lax.rem(n, 2)
        for k in range(FAR_C):
            source = far_child[k, box]
            kid_src[n * FAR_C + k] = slot_of[source // 2]
            kid_kid[n * FAR_C + k] = lax.rem(source, 2)
            kid_off[n * FAR_C + k] = far_child_off[k, box]
            kid_act[n * FAR_C + k] = jnp.where(k < far_count[box], 1.0, 0.0).astype(F32)
        return carry

    loads[0].wait()

    def phi_rows(p):
        for c in range(2):
            for k in range(2):
                xf[p, c, k, 0:50, :] = x_raw[:, k, c, p, :]

    for p in range(2):
        pl.when(core != p)(functools.partial(phi_rows, p))

    pl.semaphore_wait(barrier, 64)

    swap = pltpu.make_async_remote_copy(
        src_ref=xf.at[1 - core], dst_ref=x_swap, send_sem=s_swap.at[0], recv_sem=s_swap.at[1],
        device_id=buddy, device_id_type=MESH)
    swap.start()

    def child_start(i, carry):
        g = lax.rem(b + i, 8)

        def go(row, count, n):
            pltpu.make_async_remote_copy(
                src_ref=x_raw.at[pl.ds(group_of(g) + row, count)], dst_ref=child_recv.at[b, pl.ds(row, count)],
                send_sem=s_child.at[0, n], recv_sem=s_child.at[1, n], device_id=(g, d), device_id_type=MESH).start()

        go(0, 6, 0)

        @pl.when(g >= 6)
        def _():
            go(6, 1, 1)

        return carry

    def wait_rows(ref, first, row, count, sem):
        span = ref.at[pl.ds(0, first), pl.ds(row, count)]
        pltpu.make_async_copy(span, span, sem).wait()

    lax.fori_loop(1, 8, child_start, 0)
    child_own = pltpu.make_async_copy(x_raw.at[pl.ds(group, GROUP)], child_recv.at[b], s_loc.at[0])
    child_own.start()

    for p in range(2):
        pl.when(core == p)(functools.partial(phi_rows, p))

    lower = lax.broadcasted_iota(jnp.int32, (8, LANES), 0) < 4
    lane = lax.broadcasted_iota(jnp.int32, (8, LANES), 1)

    y_hi, x_at = j // 4, lax.rem(j, 4)
    other_box = b + 1 - 2 * lax.rem(b, 2)
    first_chip = [b * 8 + y_hi * 4, other_box * 8 + (1 - y_hi) * 4]
    rows = lax.broadcasted_iota(jnp.int32, (96, 256), 0)
    columns = lax.broadcasted_iota(jnp.int32, (96, 256), 1)
    sets = (rows >= 48).astype(jnp.int32)
    parts = (rows >> 4) - 3 * sets
    place = (rows >> 2) & 3
    theta_at = 12 * (jnp.where(rows >= 48, first_chip[1], first_chip[0]) + place) + 4 * parts + (rows & 3) - window
    swapped = theta_at + jnp.where((place & 1) == 0, 12, -12)
    picks = [(columns == q).astype(F32).astype(BF16) for q in (theta_at, swapped)]
    loads[2].wait()
    tv[...] = jnp.zeros_like(tv)

    def tab_prepare(off):
        got = []
        for c in range(2):
            tv[c, 0:100, :] = tab_raw[:, off, c, :]
            high, low = split(jnp.transpose(tv[c]))
            got.append(mul(picks[c], high) + mul(picks[c], low))
        flat = [g.reshape(12, 8, LANES) for g in got]
        even = jnp.where(lower[None], flat[0], flat[1]).reshape(2, 3, 2, 8, LANES)
        odd = jnp.where(lower[None], flat[1], flat[0]).reshape(2, 3, 2, 8, LANES)
        for s in range(2):
            for u in range(2):
                tab_send[s, 2 * u, off] = even[s, :, u]
                tab_send[s, 2 * u + 1, off] = odd[s, :, u]

    def tab_pair(pair, carry):
        tab_prepare(2 * pair)
        tab_prepare(2 * pair + 1)
        at = pl.ds(2 * pair, 2)

        def tab_start(x, carry):
            def go(s):
                box = b if s == 0 else other_box
                half = y_hi if s == 0 else 1 - y_hi
                pltpu.make_async_remote_copy(
                    src_ref=tab_send.at[s, x, at], dst_ref=tab_recv.at[core, j, at],
                    send_sem=s_tab.at[0], recv_sem=s_tab.at[1],
                    device_id=(box, (half * 4 + x) * 2 + core), device_id_type=MESH).start()

            go(1)

            @pl.when(x != x_at)
            def _():
                go(0)

            return carry

        lax.fori_loop(0, 4, tab_start, 0)
        return carry

    lax.fori_loop(0, 4, tab_pair, 0)
    tab_recv[core, j] = tab_send[0, x_at]

    swap.wait()

    def gather_rows(c, carry):
        for k in range(2):
            mine, other = xf[core, c, k, 0:50, :], x_swap[c, k, 0:50, :]
            zero = core == 0
            full = jnp.concatenate(
                [jnp.where(zero, mine, other), jnp.where(zero, other, mine), jnp.zeros((28, T_CHILD), F32)], axis=0)
            high, low = split(jnp.transpose(full))
            x_hi[c, k] = high
            x_lo[c, k] = low
        return carry

    lax.fori_loop(0, 2, gather_rows, 0)
    loads[1].wait()

    def send_all(part, count, send, recv, sems):
        def start(i, carry):
            t = lax.rem(me + i, 64)
            pltpu.make_async_remote_copy(
                src_ref=send.at[part, t, pl.ds(0, count)], dst_ref=recv.at[part, me, pl.ds(0, count)],
                send_sem=sems.at[0, part], recv_sem=sems.at[1, part], device_id=chip(t), device_id_type=MESH).start()
            return carry

        lax.fori_loop(1, 64, start, 0)
        recv[part, me] = send[part, me]

    def wait_all(part, count, ref, sem):
        span = ref.at[part, pl.ds(0, 63), pl.ds(0, count)]
        pltpu.make_async_copy(span, span, sem).wait()

    spare = (lane >= 100) & (lane < 125)

    def stow(m, tile, extra):
        shape = tile.shape
        moved = pltpu.roll(extra.reshape(-1, LANES), 100 - 25 * m, 1).reshape(shape)
        return jnp.where(spare[None], moved, tile)

    def unstow(m, tile, extra):
        shape = tile.shape
        moved = pltpu.roll(tile.reshape(-1, LANES), 28 + 25 * m, 1).reshape(shape)
        return jnp.where(((lane >= 25 * m) & (lane < 25 * m + 25))[None], moved, extra)

    def widen(part, carry):
        for c in range(2):
            got = []
            for k in range(2):
                both = mul(wide[k, part], x_hi[c, k])
                got.append(both[:256] + both[256:] + mul(wide[k, part, 0:256, :], x_lo[c, k]))
            k0 = got[0].reshape(32, 8, LANES)
            k1 = got[1].reshape(32, 8, LANES)
            m = lower[None]
            even = jnp.where(m, k0, k1)
            odd = jnp.where(m, k1, k0)
            both = jnp.stack([even, odd], axis=1).reshape(64, 8, LANES)
            send1[part, :, c * 8:c * 8 + 8, :] = both
        return carry

    lax.fori_loop(0, PARTS, widen, 0)

    def stow_forward(i, carry):
        at = pl.ds(i * 8, 8)
        extra = send1[2, at, 8:16, :]
        for m in range(4):
            half = slice(8 * (m % 2), 8 * (m % 2) + 8)
            send1[m // 2, at, half, :] = stow(m, send1[m // 2, at, half, :], extra)
        return carry

    lax.fori_loop(0, 8, stow_forward, 0)

    def send_forward(part, carry):
        send_all(part, 16, send1, recv1, s_main)
        return carry

    lax.fori_loop(0, 2, send_forward, 0)
    send_all(2, 8, send1, recv1, s_main)

    lax.fori_loop(0, 16, kid_entry, 0)
    loads[3].wait()
    for off in range(16):
        for c in range(2):
            tabc[off, c, 0:GROUP, :] = tabc_raw[:, off, c, :]
    child_own.wait()
    wait_rows(child_recv, 7, 0, 6, s_child.at[1, 0])

    @pl.when(b >= 6)
    def _():
        wait_rows(child_recv, 7, 6, 1, s_child.at[1, 1])


    def child_rows(src, carry):
        for p in range(2):
            for c in range(2):
                for k in range(2):
                    child[src, p, c, k, 0:GROUP, :] = child_recv[src, :, k, c, p, :]
        return carry

    lax.fori_loop(0, 8, child_rows, 0)

    def far_slot(s, carry):
        for kid in range(2):
            n = s * 2 + kid
            total = [[jnp.zeros((GROUP, T_CHILD), F32) for _ in range(2)] for _ in range(2)]
            for k in range(FAR_C):
                src, sk, off = kid_src[n * FAR_C + k], kid_kid[n * FAR_C + k], kid_off[n * FAR_C + k]
                act = kid_act[n * FAR_C + k]
                tr, ti = tabc[off, 0, 0:GROUP, :] * act, tabc[off, 1, 0:GROUP, :] * act
                for p in range(2):
                    xr, xi = child[src, p, 0, sk, 0:GROUP, :], child[src, p, 1, sk, 0:GROUP, :]
                    total[p][0] = total[p][0] + (tr * xr - ti * xi)
                    total[p][1] = total[p][1] + (tr * xi + ti * xr)
            for p in range(2):
                for c in range(2):
                    far_out[s, 0:GROUP, kid, c, p, :] = total[p][c]
        return carry

    lax.fori_loop(0, 8, far_slot, 0)

    def far_start(i, carry):
        to = lax.rem(b + i, 8)

        def go(row, count, n):
            pltpu.make_async_remote_copy(
                src_ref=far_out.at[to, pl.ds(row, count)], dst_ref=far_recv.at[b, pl.ds(row, count)],
                send_sem=s_far.at[0, n], recv_sem=s_far.at[1, n], device_id=(to, d), device_id_type=MESH).start()

        go(0, 6, 0)

        @pl.when(b >= 6)
        def _():
            go(6, 1, 1)

        return carry

    lax.fori_loop(1, 8, far_start, 0)
    far_own = pltpu.make_async_copy(far_out.at[b], far_recv.at[b], s_loc.at[1])
    far_own.start()

    row = lax.broadcasted_iota(jnp.int32, (8, LANES), 0)

    def shift_tables(part, carry):
        q = (12 * me + 4 * part + lax.rem(row, 4)).astype(F32)
        theta = (q + 0.5) * (math.pi / T_PARENT)
        st, ct = 16.0 * jnp.sin(theta), 16.0 * jnp.cos(theta)

        def shifts(blk, carry):
            at = pl.ds(pl.multiple_of(blk * LANES, LANES), LANES)
            ux, uy = st * angles[0, :, at], st * angles[1, :, at]
            for o in range(4):
                t = ct + (ux if o % 2 else -ux) + (uy if o // 2 else -uy)
                f = t - jnp.round(t)
                a = f * f
                s = f * (3.14159265358979 + a * (-5.16771278004997 + a * (2.55016403987735 + a * (
                    -0.599264529320792 + a * (0.0821458866111282 + a * (-0.00737043094571435
                    + a * 0.000466302805767613))))))
                c = 1.0 + a * (-4.93480220054468 + a * (4.05871212641677 + a * (-1.33526276885459 + a * (
                    0.235330630358893 + a * (-0.0258068913900141 + a * (0.00192957430940392
                    - a * 0.000104638104924846))))))
                cos, sin = 1.0 - 2.0 * (s * s), 2.0 * (s * c)
                etab[part, 4 + o, 0, :, at] = cos
                etab[part, 4 + o, 1, :, at] = sin
                etab[part, 3 - o, 0, :, at] = cos
                etab[part, 3 - o, 1, :, at] = -sin
            return carry

        lax.fori_loop(0, 16, shifts, 0)
        return carry

    lax.fori_loop(0, PARTS, shift_tables, 0)

    span = tab_recv.at[core, pl.ds(0, 7)]
    pltpu.make_async_copy(span, span, s_tab.at[1]).wait()
    tab_on = pltpu.make_async_remote_copy(
        src_ref=tab_recv.at[core], dst_ref=tab_recv.at[core], send_sem=s_tabf.at[0], recv_sem=s_tabf.at[1],
        device_id=buddy, device_id_type=MESH)
    tab_on.start()
    loads[4].wait()
    loads[6].wait()
    tab_on.wait()

    def one_part(part, carry):
        def prepare(blk, carry):
            at = pl.ds(pl.multiple_of(blk * LANES, LANES), LANES)
            dcore, dj = lax.rem(blk, 2), blk // 2
            for off in range(8):
                v = tab_recv[dcore, dj, off, part]
                w = pltpu.roll(v, 4, 0)
                one = jnp.where(lower, v, w)
                two = jnp.where(lower, w, v)
                tab[off, 0, :, at] = jnp.where(chip_odd, two, one)
                tab[off, 1, :, at] = jnp.where(chip_odd, one, two)
            return carry

        lax.fori_loop(0, 16, prepare, 0)

        @pl.when(part < 2)
        def _():
            wait_all(part, 16, recv1, s_main.at[1, part])

        @pl.when(part == 2)
        def _():
            wait_all(2, 8, recv1, s_main.at[1, 2])

            def take(i, carry):
                at = pl.ds(i * 8, 8)
                extra = jnp.zeros((8, 8, LANES), F32)
                for m in range(4):
                    extra = unstow(m, recv1[m // 2, at, 8 * (m % 2):8 * (m % 2) + 8, :], extra)
                recv1[2, at, 8:16, :] = extra
                return carry

            lax.fori_loop(0, 8, take, 0)

        got = recv1[part].reshape(8, 8, 16, LANES)
        for sign in range(2):
            pieces = []
            for jj in range(4):
                one, two = got[:, jj], got[:, jj + 4]
                pieces.append((one + two if sign == 0 else one - two).reshape(128, LANES))
            both = jnp.concatenate(split(jnp.concatenate(pieces, axis=1)), axis=0)
            for n in range(4):
                cols = slice(n * 256, n * 256 + 256)
                wh, wl = weights[sign, 0, :, cols], weights[sign, 1, :, cols]
                y[sign, :, cols] = mul_rows(both, wh, wl)

        def block(dd, carry):
            for half in range(2):
                at_y = pl.ds(pl.multiple_of(dd * LANES, LANES), LANES)
                at = pl.ds(pl.multiple_of((dd + 8 * half) * LANES, LANES), LANES)
                for s in range(8):
                    yp = y[0, s * 16:s * 16 + 16, at_y]
                    ym = y[1, s * 16:s * 16 + 16, at_y]
                    v = yp + ym if half == 0 else yp - ym
                    vr, vi = v[:8], v[8:]
                    cos = jnp.where(lower, etab[part, oct_lo[s], 0, :, at], etab[part, oct_hi[s], 0, :, at])
                    sin = jnp.where(lower, etab[part, oct_lo[s], 1, :, at], etab[part, oct_hi[s], 1, :, at])
                    re = cos * vr - sin * vi
                    im = sin * vr + cos * vi
                    pr[half, s, 0] = re + pltpu.roll(re, 4, 0)
                    pr[half, s, 1] = im + pltpu.roll(im, 4, 0)
            for s in range(8):
                back = []
                for half in range(2):
                    at = pl.ds(pl.multiple_of((dd + 8 * half) * LANES, LANES), LANES)
                    re = im = None
                    for k in range(FAR_P):
                        src, off = par_src[s * FAR_P + k], par_off[s * FAR_P + k]
                        fr, fi = pr[half, src, 0], pr[half, src, 1]
                        tr, ti = tab[off, 0, :, at], tab[off, 1, :, at]
                        gr, gi = tr * fr - ti * fi, tr * fi + ti * fr
                        re = gr if re is None else re + gr
                        im = gi if im is None else im + gi
                    cos = jnp.where(lower, etab[part, oct_lo[s], 0, :, at], etab[part, oct_hi[s], 0, :, at])
                    sin = jnp.where(lower, etab[part, oct_lo[s], 1, :, at], etab[part, oct_hi[s], 1, :, at])
                    back.append(jnp.concatenate([cos * re + sin * im, cos * im - sin * re], axis=0))
                at_y = pl.ds(pl.multiple_of(dd * LANES, LANES), LANES)
                for sign in range(2):
                    high, low = split(back[0] + back[1] if sign == 0 else back[0] - back[1])
                    r[sign, s * 16:s * 16 + 16, at_y] = high
                    r[sign, 128 + s * 16:144 + s * 16, at_y] = low
            return carry

        lax.fori_loop(0, 8, block, 0)

        for n in range(2):
            cols = slice(n * 256, n * 256 + 256)
            z = [mul_rows(r[sign], weights_back[sign, 0, :, cols], weights_back[sign, 1, :, cols])
                 for sign in range(2)]
            one, two = z[0] + z[1], z[0] - z[1]
            for h in range(2):
                a = one[:, h * LANES:h * LANES + LANES].reshape(8, 16, LANES)
                c = two[:, h * LANES:h * LANES + LANES].reshape(8, 16, LANES)
                for s in range(8):
                    send2[part, s * 8 + 2 * n + h] = a[s]
                    send2[part, s * 8 + 2 * n + h + 4] = c[s]

        for at_part in range(PARTS):
            @pl.when(part == at_part)
            def _():
                if at_part > 0:
                    def stow_back(i, carry):
                        at = pl.ds(i * 8, 8)
                        extra = send2[0, at, 8:16, :]
                        for h in range(2):
                            half = slice(8 * h, 8 * h + 8)
                            send2[at_part, at, half, :] = stow(
                                2 * at_part - 2 + h, send2[at_part, at, half, :], extra)
                        return carry

                    lax.fori_loop(0, 8, stow_back, 0)
                send_all(at_part, 16 if at_part > 0 else 8, send2, recv2, s_back)

        return carry

    lax.fori_loop(0, PARTS, one_part, 0)

    far_own.wait()
    wait_rows(far_recv, 7, 0, 6, s_far.at[1, 0])

    @pl.when(b >= 6)
    def _():
        wait_rows(far_recv, 1, 6, 1, s_far.at[1, 1])

    @pl.when(b < 6)
    def _():
        wait_rows(far_recv, 2, 6, 1, s_far.at[1, 1])

    for p in range(2):
        for c in range(2):
            for k in range(2):
                for g in range(8):
                    first, count = 6 * g + max(g - 6, 0), 6 + (g >= 6)
                    far[p, c, k, first:first + count, :] = far_recv[g, 0:count, k, c, p, :]

    loads[5].wait()
    acc[...] = jnp.zeros_like(acc)

    def narrow_tile(part, c):
        got = recv2[part, :, c * 8:c * 8 + 8, :].reshape(32, 2, 8, LANES)
        even, odd = got[:, 0], got[:, 1]
        m = lower[None]
        for k in range(2):
            rows = jnp.where(m, even, odd) if k == 0 else jnp.where(m, odd, even)
            high, low = split(rows.reshape(256, LANES))
            both = mul(narrow[k, part], high)
            acc[c, k] = acc[c, k] + (both[:T_CHILD] + both[T_CHILD:] + mul(narrow[k, part, 0:T_CHILD, :], low))

    wait_all(0, 8, recv2, s_back.at[1, 0])
    narrow_tile(0, 0)

    def hand_over(c):
        return pltpu.make_async_remote_copy(
            src_ref=own.at[1 - core, c], dst_ref=res_recv.at[c], send_sem=s_swap.at[2 + c], recv_sem=s_swap.at[4 + c],
            device_id=buddy, device_id_type=MESH)

    def finish(c):
        for k in range(2):
            full = jnp.transpose(acc[c, k])
            own[0, c, k, 0:50, :] = full[0:50]
            own[1, c, k, 0:50, :] = full[50:100]
        hand_over(c).start()

    def keep(c):
        for p in range(2):
            @pl.when(core == p)
            def _():
                for k in range(2):
                    out[:, k, c, p, :] = own[p, c, k, 0:50, :] + far[p, c, k, 0:50, :]

    def take_over(c):
        hand_over(c).wait()
        for p in range(2):
            @pl.when(core != p)
            def _():
                for k in range(2):
                    out[:, k, c, p, :] = res_recv[c, k, 0:50, :] + far[p, c, k, 0:50, :]

    wait_all(1, 16, recv2, s_back.at[1, 1])
    narrow_tile(1, 0)
    narrow_tile(1, 1)
    wait_all(2, 16, recv2, s_back.at[1, 2])
    narrow_tile(2, 0)
    finish(0)

    def take_back(i, carry):
        at = pl.ds(i * 8, 8)
        extra = jnp.zeros((8, 8, LANES), F32)
        for m in range(4):
            extra = unstow(m, recv2[1 + m // 2, at, 8 * (m % 2):8 * (m % 2) + 8, :], extra)
        recv2[0, at, 8:16, :] = extra
        return carry

    lax.fori_loop(0, 8, take_back, 0)
    narrow_tile(2, 1)
    narrow_tile(0, 1)
    finish(1)
    keep(0)
    keep(1)
    take_over(0)
    take_over(1)

    for part in range(PARTS):
        wait_all(part, 8 if part == 2 else 16, send1, s_main.at[0, part])
        wait_all(part, 8 if part == 0 else 16, send2, s_back.at[0, part])
    wait_rows(child_recv, 7, 0, 6, s_child.at[0, 0])
    wait_rows(far_recv, 7, 0, 6, s_far.at[0, 0])

    @pl.when(b >= 6)
    def _():
        wait_rows(child_recv, 1, 6, 1, s_child.at[0, 1])
        wait_rows(far_recv, 7, 6, 1, s_far.at[0, 1])

    @pl.when(b < 6)
    def _():
        wait_rows(child_recv, 2, 6, 1, s_child.at[0, 1])

    span = tab_recv.at[core, pl.ds(0, 7)]
    pltpu.make_async_copy(span, span, s_tab.at[0]).wait()


def shards(child_rad, box_at_slot, octant, far_par, far_par_off, far_child, far_child_off, far_child_count,
           trans_par, trans_child):
    wide, narrow = theta_tables()
    vmem = pl.BlockSpec(memory_space=pltpu.VMEM)
    smem = pl.BlockSpec(memory_space=pltpu.SMEM)
    anywhere = pl.BlockSpec(memory_space=pl.ANY)
    chunks = pltpu.VMEM((PARTS, 64, 16, LANES), F32)
    groups = pltpu.VMEM((8, GROUP, 2, 2, 2, T_CHILD), F32)
    there, back = phi_tables()
    out = pl.pallas_call(
        kernel,
        out_shape=pltpu.VMEM((50, 2, 2, 2, T_CHILD), F32),
        in_specs=[smem] * 7 + [anywhere] * 7 + [vmem],
        out_specs=vmem,
        scratch_shapes=[
            pltpu.SMEM((8,), jnp.int32),
            pltpu.SMEM((8,), jnp.int32),
            pltpu.SMEM((8,), jnp.int32),
            pltpu.SMEM((24,), jnp.int32),
            pltpu.SMEM((24,), jnp.int32),
            pltpu.SMEM((112,), jnp.int32),
            pltpu.SMEM((112,), jnp.int32),
            pltpu.SMEM((112,), jnp.int32),
            pltpu.SMEM((112,), F32),
            pltpu.VMEM((50, 2, 2, 2, T_CHILD), F32),
            pltpu.VMEM((100, 8, 2, 256), F32),
            pltpu.VMEM((GROUP, 16, 2, T_CHILD), F32),
            pltpu.VMEM(wide.shape, BF16),
            pltpu.VMEM(narrow.shape, BF16),
            pltpu.VMEM(there.shape, BF16),
            pltpu.VMEM(back.shape, BF16),
            pltpu.VMEM((2, 2, 2, 56, T_CHILD), F32),
            pltpu.VMEM((2, 2, 56, T_CHILD), F32),
            pltpu.VMEM((2, 2, T_CHILD, LANES), BF16),
            pltpu.VMEM((2, 2, T_CHILD, LANES), BF16),
            chunks, chunks, chunks, chunks,
            groups,
            pltpu.VMEM((8, 2, 2, 2, 8, T_CHILD), F32),
            pltpu.VMEM((16, 2, 8, T_CHILD), F32),
            groups,
            groups,
            pltpu.VMEM((2, 2, 2, 56, T_CHILD), F32),
            pltpu.VMEM((2, LANES, 256), F32),
            pltpu.VMEM((2, 4, 8, PARTS, 8, LANES), F32),
            pltpu.VMEM((2, 8, 8, PARTS, 8, LANES), F32),
            pltpu.VMEM((8, 2, 8, 16 * LANES), F32),
            pltpu.VMEM((PARTS, 8, 2, 8, 16 * LANES), F32),
            pltpu.VMEM((2, 128, 8 * LANES), F32),
            pltpu.VMEM((2, 8, 2, 8, LANES), F32),
            pltpu.VMEM((2, 256, 8 * LANES), BF16),
            pltpu.VMEM((2, 2, T_CHILD, LANES), F32),
            pltpu.VMEM((2, 2, 2, 56, T_CHILD), F32),
            pltpu.VMEM((2, 2, 56, T_CHILD), F32),
            pltpu.SemaphoreType.DMA((7,)),
            pltpu.SemaphoreType.DMA((6,)),
            pltpu.SemaphoreType.DMA((2, 2)),
            pltpu.SemaphoreType.DMA((2, 2)),
            pltpu.SemaphoreType.DMA((2,)),
            pltpu.SemaphoreType.DMA((2,)),
            pltpu.SemaphoreType.DMA((2, PARTS)),
            pltpu.SemaphoreType.DMA((2, PARTS)),
            pltpu.SemaphoreType.DMA((2,)),
        ],
        compiler_params=pltpu.CompilerParams(
            collective_id=0, has_side_effects=True, vmem_limit_bytes=60 * 2**20),
        cost_estimate=pl.CostEstimate(flops=14_000_000_000, bytes_accessed=16_000_000, transcendentals=0),
        name="fields",
    )(box_at_slot, octant, far_par.T, far_par_off.T, far_child.T, far_child_off.T, far_child_count,
      child_rad, trans_par, trans_child,
      jnp.asarray(wide), jnp.asarray(narrow), jnp.asarray(there), jnp.asarray(back), jnp.asarray(phi_angles()))
    return out


def solution(mesh):
    return jax.shard_map(
        shards,
        mesh=mesh,
        in_specs=(P("dir", "box", None, None, None), P(), P(), P(), P(), P(), P(), P(),
                  P("dir", None, None, None), P("dir", None, None, None)),
        out_specs=P("dir", "box", None, None, None),
        check_vma=False,
    )
```

```python
import functools
import math

import jax
import jax.numpy as jnp
import numpy as np
from jax import lax
from jax.experimental import pallas as pl
from jax.experimental.pallas import tpu as pltpu
from jax.sharding import PartitionSpec as P

T_CHILD, P_CHILD = 384, 800
T_PARENT, P_PARENT = 768, 1600
FAR_P, FAR_C = 3, 7

PARTS = 3
LANES = 128
GROUP = 7
MESH = pl.DeviceIdType.MESH
F32, BF16 = jnp.float32, jnp.bfloat16


def split_np(table):
    high = table.astype(np.float32).astype(jnp.bfloat16)
    low = (table - high.astype(np.float64)).astype(np.float32).astype(jnp.bfloat16)
    return high, low


@functools.cache
def theta_tables():
    q = np.arange(T_PARENT)
    first = np.clip((q - 1) // 2 - 2, 0, T_CHILD - 6)
    offset = q * 0.5 - 0.25 - first
    table = np.zeros((T_PARENT, T_CHILD))
    for node in range(6):
        weight = np.ones(T_PARENT)
        for other in range(6):
            if other != node:
                weight = weight * (offset - other) / (node - other)
        table[q, first + node] = weight
    part, pair, place, i = np.meshgrid(np.arange(PARTS), np.arange(32), np.arange(2), np.arange(4), indexing="ij")
    wide, narrow = [], []
    for kid in range(2):
        chip = 2 * pair + (place if kid == 0 else 1 - place)
        rows = table[(12 * chip + 4 * part + i).reshape(-1)]
        rows = rows.reshape(PARTS, 256, T_CHILD)
        wide.append(np.concatenate(split_np(rows), axis=1))
        narrow.append(np.concatenate(split_np(0.25 * rows.transpose(0, 2, 1)), axis=1))
    return np.stack(wide), np.stack(narrow)


@functools.cache
def phi_tables():
    p = np.arange(P_PARENT)[:, None]
    c = np.arange(P_CHILD)[None, :]
    odd = 2 * p - 4 * c - 1
    period = 4 * P_CHILD
    numerator = np.mod((P_CHILD - 1) * odd, 2 * period).astype(np.float64)
    table = np.sin(math.pi * numerator / period) / (P_CHILD * np.sin(math.pi * odd / period))
    plus = np.zeros((4 * LANES, 8 * LANES))
    minus = np.zeros((4 * LANES, 8 * LANES))
    f = np.arange(50)
    for jj in range(4):
        for core in range(2):
            child = 100 * jj + 50 * core + f
            rows = jj * LANES + core * 50 + f
            for dd in range(8):
                parent = 100 * dd + np.arange(100)
                near = table[np.ix_(parent, child)].T
                far = table[np.ix_(parent, child + 400)].T
                at = np.ix_(rows, dd * LANES + np.arange(100))
                plus[at] = 0.5 * (near + far)
                minus[at] = 0.5 * (near - far)
    there = np.stack([np.stack(split_np(plus)), np.stack(split_np(minus))])
    return there, np.ascontiguousarray(there.transpose(0, 1, 3, 2))


@functools.cache
def phi_angles():
    lane = np.arange(16 * LANES)
    phi = 2.0 * math.pi * (100 * (lane // LANES) + lane % LANES + 0.5) / P_PARENT
    return np.stack([np.cos(phi), np.sin(phi)]).reshape(2, 1, 16 * LANES).astype(np.float32)


def split(x):
    high = x.astype(BF16)
    return high, (x - high.astype(F32)).astype(BF16)


def mul(a, b):
    return jnp.dot(a, b, preferred_element_type=F32)


def mul_rows(both, w_high, w_low):
    n = both.shape[0] // 2
    got = mul(both, w_high)
    return got[:n] + got[n:] + mul(both[:n], w_low)


def kernel(
    bas, octant, far_par, far_par_off, far_child, far_child_off, far_count,
    x_hbm, tab_hbm, tabc_hbm, wide_hbm, narrow_hbm, weights_hbm, back_hbm, angles,
    out,
    slot_of, oct_lo, oct_hi, par_src, par_off, kid_src, kid_kid, kid_off, kid_act,
    x_raw, tab_raw, tabc_raw, wide, narrow, weights, weights_back,
    xf, x_swap, x_hi, x_lo, send1, recv1, send2, recv2,
    child_recv, child, tabc, far_out, far_recv, far, tv, tab_send, tab_recv, tab, etab, y, pr, r, acc, own,
    res_recv,
    s_in, s_swap, s_child, s_far, s_tab, s_tabf, s_main, s_back, s_loc,
):
    b = lax.axis_index("box")
    d = lax.axis_index("dir")
    core = lax.rem(d, 2)
    j = d // 2
    me = b * 8 + j
    chip_odd = lax.rem(j, 2) == 1
    buddy = (b, d + 1 - 2 * core)

    def chip(t):
        return (t // 8, lax.rem(t, 8) * 2 + core)

    barrier = pltpu.get_barrier_semaphore()
    pl.semaphore_signal(barrier, inc=1, device_id=buddy, device_id_type=MESH)

    def greet(i, carry):
        pl.semaphore_signal(barrier, inc=1, device_id=chip(lax.rem(me + i, 64)), device_id_type=MESH)
        return carry

    def group_of(g):
        return 6 * g + jnp.maximum(g - 6, 0)

    group = group_of(b)
    window = pl.multiple_of((3 * (b // 2)) // 2 * LANES, LANES)
    loads = [
        pltpu.make_async_copy(x_hbm, x_raw, s_in.at[0]),
        pltpu.make_async_copy(wide_hbm, wide, s_in.at[1]),
        pltpu.make_async_copy(tab_hbm.at[:, :, :, pl.ds(window, 256)], tab_raw, s_in.at[2]),
        pltpu.make_async_copy(tabc_hbm.at[pl.ds(group, GROUP)], tabc_raw, s_in.at[3]),
        pltpu.make_async_copy(weights_hbm, weights, s_in.at[4]),
        pltpu.make_async_copy(narrow_hbm, narrow, s_in.at[5]),
        pltpu.make_async_copy(back_hbm, weights_back, s_in.at[6]),
    ]
    loads[0].start()
    lax.fori_loop(1, 64, greet, 0)
    for load in loads[1:]:
        load.start()

    for box in range(8):
        place = jnp.int32(0)
        for s in range(8):
            place = jnp.where(bas[s] == box, s, place)
        slot_of[box] = place
    for s in range(8):
        box = bas[s]
        o0, o1 = octant[2 * box], octant[2 * box + 1]
        oct_lo[s] = jnp.where(chip_odd, o1, o0)
        oct_hi[s] = jnp.where(chip_odd, o0, o1)
        for k in range(FAR_P):
            par_src[s * FAR_P + k] = slot_of[far_par[k, box]]
            par_off[s * FAR_P + k] = far_par_off[k, box]

    def kid_entry(n, carry):
        box = bas[n // 2] * 2 + lax.rem(n, 2)
        for k in range(FAR_C):
            source = far_child[k, box]
            kid_src[n * FAR_C + k] = slot_of[source // 2]
            kid_kid[n * FAR_C + k] = lax.rem(source, 2)
            kid_off[n * FAR_C + k] = far_child_off[k, box]
            kid_act[n * FAR_C + k] = jnp.where(k < far_count[box], 1.0, 0.0).astype(F32)
        return carry

    loads[0].wait()

    def phi_rows(p):
        for c in range(2):
            for k in range(2):
                xf[p, c, k, 0:50, :] = x_raw[:, k, c, p, :]

    for p in range(2):
        pl.when(core != p)(functools.partial(phi_rows, p))

    pl.semaphore_wait(barrier, 64)

    swap = pltpu.make_async_remote_copy(
        src_ref=xf.at[1 - core], dst_ref=x_swap, send_sem=s_swap.at[0], recv_sem=s_swap.at[1],
        device_id=buddy, device_id_type=MESH)
    swap.start()

    def child_start(i, carry):
        g = lax.rem(b + i, 8)

        def go(row, count, n):
            pltpu.make_async_remote_copy(
                src_ref=x_raw.at[pl.ds(group_of(g) + row, count)], dst_ref=child_recv.at[b, pl.ds(row, count)],
                send_sem=s_child.at[0, n], recv_sem=s_child.at[1, n], device_id=(g, d), device_id_type=MESH).start()

        go(0, 6, 0)

        @pl.when(g >= 6)
        def _():
            go(6, 1, 1)

        return carry

    def wait_rows(ref, first, row, count, sem):
        span = ref.at[pl.ds(0, first), pl.ds(row, count)]
        pltpu.make_async_copy(span, span, sem).wait()

    lax.fori_loop(1, 8, child_start, 0)
    child_own = pltpu.make_async_copy(x_raw.at[pl.ds(group, GROUP)], child_recv.at[b], s_loc.at[0])
    child_own.start()

    for p in range(2):
        pl.when(core == p)(functools.partial(phi_rows, p))

    lower = lax.broadcasted_iota(jnp.int32, (8, LANES), 0) < 4
    lane = lax.broadcasted_iota(jnp.int32, (8, LANES), 1)

    y_hi, x_at = j // 4, lax.rem(j, 4)
    other_box = b + 1 - 2 * lax.rem(b, 2)
    first_chip = [b * 8 + y_hi * 4, other_box * 8 + (1 - y_hi) * 4]
    rows = lax.broadcasted_iota(jnp.int32, (96, 256), 0)
    columns = lax.broadcasted_iota(jnp.int32, (96, 256), 1)
    sets = (rows >= 48).astype(jnp.int32)
    parts = (rows >> 4) - 3 * sets
    place = (rows >> 2) & 3
    theta_at = 12 * (jnp.where(rows >= 48, first_chip[1], first_chip[0]) + place) + 4 * parts + (rows & 3) - window
    swapped = theta_at + jnp.where((place & 1) == 0, 12, -12)
    picks = [(columns == q).astype(F32).astype(BF16) for q in (theta_at, swapped)]
    loads[2].wait()
    tv[...] = jnp.zeros_like(tv)

    def tab_prepare(off):
        got = []
        for c in range(2):
            tv[c, 0:100, :] = tab_raw[:, off, c, :]
            high, low = split(jnp.transpose(tv[c]))
            got.append(mul(picks[c], high) + mul(picks[c], low))
        flat = [g.reshape(12, 8, LANES) for g in got]
        even = jnp.where(lower[None], flat[0], flat[1]).reshape(2, 3, 2, 8, LANES)
        odd = jnp.where(lower[None], flat[1], flat[0]).reshape(2, 3, 2, 8, LANES)
        for s in range(2):
            for u in range(2):
                tab_send[s, 2 * u, off] = even[s, :, u]
                tab_send[s, 2 * u + 1, off] = odd[s, :, u]

    def tab_pair(pair, carry):
        tab_prepare(2 * pair)
        tab_prepare(2 * pair + 1)
        at = pl.ds(2 * pair, 2)

        def tab_start(x, carry):
            def go(s):
                box = b if s == 0 else other_box
                half = y_hi if s == 0 else 1 - y_hi
                pltpu.make_async_remote_copy(
                    src_ref=tab_send.at[s, x, at], dst_ref=tab_recv.at[core, j, at],
                    send_sem=s_tab.at[0], recv_sem=s_tab.at[1],
                    device_id=(box, (half * 4 + x) * 2 + core), device_id_type=MESH).start()

            go(1)

            @pl.when(x != x_at)
            def _():
                go(0)

            return carry

        lax.fori_loop(0, 4, tab_start, 0)
        return carry

    lax.fori_loop(0, 4, tab_pair, 0)
    tab_recv[core, j] = tab_send[0, x_at]

    swap.wait()

    def gather_rows(c, carry):
        for k in range(2):
            mine, other = xf[core, c, k, 0:50, :], x_swap[c, k, 0:50, :]
            zero = core == 0
            full = jnp.concatenate(
                [jnp.where(zero, mine, other), jnp.where(zero, other, mine), jnp.zeros((28, T_CHILD), F32)], axis=0)
            high, low = split(jnp.transpose(full))
            x_hi[c, k] = high
            x_lo[c, k] = low
        return carry

    lax.fori_loop(0, 2, gather_rows, 0)
    loads[1].wait()

    def send_all(part, count, send, recv, sems):
        def start(i, carry):
            t = lax.rem(me + i, 64)
            pltpu.make_async_remote_copy(
                src_ref=send.at[part, t, pl.ds(0, count)], dst_ref=recv.at[part, me, pl.ds(0, count)],
                send_sem=sems.at[0, part], recv_sem=sems.at[1, part], device_id=chip(t), device_id_type=MESH).start()
            return carry

        lax.fori_loop(1, 64, start, 0)
        recv[part, me] = send[part, me]

    def wait_all(part, count, ref, sem):
        span = ref.at[part, pl.ds(0, 63), pl.ds(0, count)]
        pltpu.make_async_copy(span, span, sem).wait()

    spare = (lane >= 100) & (lane < 125)

    def stow(m, tile, extra):
        shape = tile.shape
        moved = pltpu.roll(extra.reshape(-1, LANES), 100 - 25 * m, 1).reshape(shape)
        return jnp.where(spare[None], moved, tile)

    def unstow(m, tile, extra):
        shape = tile.shape
        moved = pltpu.roll(tile.reshape(-1, LANES), 28 + 25 * m, 1).reshape(shape)
        return jnp.where(((lane >= 25 * m) & (lane < 25 * m + 25))[None], moved, extra)

    def widen(part, carry):
        for c in range(2):
            got = []
            for k in range(2):
                both = mul(wide[k, part], x_hi[c, k])
                got.append(both[:256] + both[256:] + mul(wide[k, part, 0:256, :], x_lo[c, k]))
            k0 = got[0].reshape(32, 8, LANES)
            k1 = got[1].reshape(32, 8, LANES)
            m = lower[None]
            even = jnp.where(m, k0, k1)
            odd = jnp.where(m, k1, k0)
            both = jnp.stack([even, odd], axis=1).reshape(64, 8, LANES)
            send1[part, :, c * 8:c * 8 + 8, :] = both
        return carry

    lax.fori_loop(0, PARTS, widen, 0)

    def stow_forward(i, carry):
        at = pl.ds(i * 8, 8)
        extra = send1[2, at, 8:16, :]
        for m in range(4):
            half = slice(8 * (m % 2), 8 * (m % 2) + 8)
            send1[m // 2, at, half, :] = stow(m, send1[m // 2, at, half, :], extra)
        return carry

    lax.fori_loop(0, 8, stow_forward, 0)

    def send_forward(part, carry):
        send_all(part, 16, send1, recv1, s_main)
        return carry

    lax.fori_loop(0, 2, send_forward, 0)
    send_all(2, 8, send1, recv1, s_main)

    lax.fori_loop(0, 16, kid_entry, 0)
    loads[3].wait()
    for off in range(16):
        for c in range(2):
            tabc[off, c, 0:GROUP, :] = tabc_raw[:, off, c, :]
    child_own.wait()
    wait_rows(child_recv, 7, 0, 6, s_child.at[1, 0])

    @pl.when(b >= 6)
    def _():
        wait_rows(child_recv, 7, 6, 1, s_child.at[1, 1])


    def child_rows(src, carry):
        for p in range(2):
            for c in range(2):
                for k in range(2):
                    child[src, p, c, k, 0:GROUP, :] = child_recv[src, :, k, c, p, :]
        return carry

    lax.fori_loop(0, 8, child_rows, 0)

    def far_slot(s, carry):
        for kid in range(2):
            n = s * 2 + kid
            total = [[jnp.zeros((GROUP, T_CHILD), F32) for _ in range(2)] for _ in range(2)]
            for k in range(FAR_C):
                src, sk, off = kid_src[n * FAR_C + k], kid_kid[n * FAR_C + k], kid_off[n * FAR_C + k]
                act = kid_act[n * FAR_C + k]
                tr, ti = tabc[off, 0, 0:GROUP, :] * act, tabc[off, 1, 0:GROUP, :] * act
                for p in range(2):
                    xr, xi = child[src, p, 0, sk, 0:GROUP, :], child[src, p, 1, sk, 0:GROUP, :]
                    total[p][0] = total[p][0] + (tr * xr - ti * xi)
                    total[p][1] = total[p][1] + (tr * xi + ti * xr)
            for p in range(2):
                for c in range(2):
                    far_out[s, 0:GROUP, kid, c, p, :] = total[p][c]
        return carry

    lax.fori_loop(0, 8, far_slot, 0)

    def far_start(i, carry):
        to = lax.rem(b + i, 8)

        def go(row, count, n):
            pltpu.make_async_remote_copy(
                src_ref=far_out.at[to, pl.ds(row, count)], dst_ref=far_recv.at[b, pl.ds(row, count)],
                send_sem=s_far.at[0, n], recv_sem=s_far.at[1, n], device_id=(to, d), device_id_type=MESH).start()

        go(0, 6, 0)

        @pl.when(b >= 6)
        def _():
            go(6, 1, 1)

        return carry

    lax.fori_loop(1, 8, far_start, 0)
    far_own = pltpu.make_async_copy(far_out.at[b], far_recv.at[b], s_loc.at[1])
    far_own.start()

    row = lax.broadcasted_iota(jnp.int32, (8, LANES), 0)

    def shift_tables(part, carry):
        q = (12 * me + 4 * part + lax.rem(row, 4)).astype(F32)
        theta = (q + 0.5) * (math.pi / T_PARENT)
        st, ct = 16.0 * jnp.sin(theta), 16.0 * jnp.cos(theta)

        def shifts(blk, carry):
            at = pl.ds(pl.multiple_of(blk * LANES, LANES), LANES)
            ux, uy = st * angles[0, :, at], st * angles[1, :, at]
            for o in range(4):
                t = ct + (ux if o % 2 else -ux) + (uy if o // 2 else -uy)
                f = t - jnp.round(t)
                a = f * f
                s = f * (3.14159265358979 + a * (-5.16771278004997 + a * (2.55016403987735 + a * (
                    -0.599264529320792 + a * (0.0821458866111282 + a * (-0.00737043094571435
                    + a * 0.000466302805767613))))))
                c = 1.0 + a * (-4.93480220054468 + a * (4.05871212641677 + a * (-1.33526276885459 + a * (
                    0.235330630358893 + a * (-0.0258068913900141 + a * (0.00192957430940392
                    - a * 0.000104638104924846))))))
                cos, sin = 1.0 - 2.0 * (s * s), 2.0 * (s * c)
                etab[part, 4 + o, 0, :, at] = cos
                etab[part, 4 + o, 1, :, at] = sin
                etab[part, 3 - o, 0, :, at] = cos
                etab[part, 3 - o, 1, :, at] = -sin
            return carry

        lax.fori_loop(0, 16, shifts, 0)
        return carry

    lax.fori_loop(0, PARTS, shift_tables, 0)

    span = tab_recv.at[core, pl.ds(0, 7)]
    pltpu.make_async_copy(span, span, s_tab.at[1]).wait()
    tab_on = pltpu.make_async_remote_copy(
        src_ref=tab_recv.at[core], dst_ref=tab_recv.at[core], send_sem=s_tabf.at[0], recv_sem=s_tabf.at[1],
        device_id=buddy, device_id_type=MESH)
    tab_on.start()
    loads[4].wait()
    loads[6].wait()
    tab_on.wait()

    def one_part(part, carry):
        def prepare(blk, carry):
            at = pl.ds(pl.multiple_of(blk * LANES, LANES), LANES)
            dcore, dj = lax.rem(blk, 2), blk // 2
            for off in range(8):
                v = tab_recv[dcore, dj, off, part]
                w = pltpu.roll(v, 4, 0)
                one = jnp.where(lower, v, w)
                two = jnp.where(lower, w, v)
                tab[off, 0, :, at] = jnp.where(chip_odd, two, one)
                tab[off, 1, :, at] = jnp.where(chip_odd, one, two)
            return carry

        lax.fori_loop(0, 16, prepare, 0)

        @pl.when(part < 2)
        def _():
            wait_all(part, 16, recv1, s_main.at[1, part])

        @pl.when(part == 2)
        def _():
            wait_all(2, 8, recv1, s_main.at[1, 2])

            def take(i, carry):
                at = pl.ds(i * 8, 8)
                extra = jnp.zeros((8, 8, LANES), F32)
                for m in range(4):
                    extra = unstow(m, recv1[m // 2, at, 8 * (m % 2):8 * (m % 2) + 8, :], extra)
                recv1[2, at, 8:16, :] = extra
                return carry

            lax.fori_loop(0, 8, take, 0)

        got = recv1[part].reshape(8, 8, 16, LANES)
        for sign in range(2):
            pieces = []
            for jj in range(4):
                one, two = got[:, jj], got[:, jj + 4]
                pieces.append((one + two if sign == 0 else one - two).reshape(128, LANES))
            both = jnp.concatenate(split(jnp.concatenate(pieces, axis=1)), axis=0)
            for n in range(4):
                cols = slice(n * 256, n * 256 + 256)
                wh, wl = weights[sign, 0, :, cols], weights[sign, 1, :, cols]
                y[sign, :, cols] = mul_rows(both, wh, wl)

        def block(dd, carry):
            for half in range(2):
                at_y = pl.ds(pl.multiple_of(dd * LANES, LANES), LANES)
                at = pl.ds(pl.multiple_of((dd + 8 * half) * LANES, LANES), LANES)
                for s in range(8):
                    yp = y[0, s * 16:s * 16 + 16, at_y]
                    ym = y[1, s * 16:s * 16 + 16, at_y]
                    v = yp + ym if half == 0 else yp - ym
                    vr, vi = v[:8], v[8:]
                    cos = jnp.where(lower, etab[part, oct_lo[s], 0, :, at], etab[part, oct_hi[s], 0, :, at])
                    sin = jnp.where(lower, etab[part, oct_lo[s], 1, :, at], etab[part, oct_hi[s], 1, :, at])
                    re = cos * vr - sin * vi
                    im = sin * vr + cos * vi
                    pr[half, s, 0] = re + pltpu.roll(re, 4, 0)
                    pr[half, s, 1] = im + pltpu.roll(im, 4, 0)
            for s in range(8):
                back = []
                for half in range(2):
                    at = pl.ds(pl.multiple_of((dd + 8 * half) * LANES, LANES), LANES)
                    re = im = None
                    for k in range(FAR_P):
                        src, off = par_src[s * FAR_P + k], par_off[s * FAR_P + k]
                        fr, fi = pr[half, src, 0], pr[half, src, 1]
                        tr, ti = tab[off, 0, :, at], tab[off, 1, :, at]
                        gr, gi = tr * fr - ti * fi, tr * fi + ti * fr
                        re = gr if re is None else re + gr
                        im = gi if im is None else im + gi
                    cos = jnp.where(lower, etab[part, oct_lo[s], 0, :, at], etab[part, oct_hi[s], 0, :, at])
                    sin = jnp.where(lower, etab[part, oct_lo[s], 1, :, at], etab[part, oct_hi[s], 1, :, at])
                    back.append(jnp.concatenate([cos * re + sin * im, cos * im - sin * re], axis=0))
                at_y = pl.ds(pl.multiple_of(dd * LANES, LANES), LANES)
                for sign in range(2):
                    high, low = split(back[0] + back[1] if sign == 0 else back[0] - back[1])
                    r[sign, s * 16:s * 16 + 16, at_y] = high
                    r[sign, 128 + s * 16:144 + s * 16, at_y] = low
            return carry

        lax.fori_loop(0, 8, block, 0)

        for n in range(2):
            cols = slice(n * 256, n * 256 + 256)
            z = [mul_rows(r[sign], weights_back[sign, 0, :, cols], weights_back[sign, 1, :, cols])
                 for sign in range(2)]
            one, two = z[0] + z[1], z[0] - z[1]
            for h in range(2):
                a = one[:, h * LANES:h * LANES + LANES].reshape(8, 16, LANES)
                c = two[:, h * LANES:h * LANES + LANES].reshape(8, 16, LANES)
                for s in range(8):
                    send2[part, s * 8 + 2 * n + h] = a[s]
                    send2[part, s * 8 + 2 * n + h + 4] = c[s]

        for at_part in range(PARTS):
            @pl.when(part == at_part)
            def _():
                if at_part > 0:
                    def stow_back(i, carry):
                        at = pl.ds(i * 8, 8)
                        extra = send2[0, at, 8:16, :]
                        for h in range(2):
                            half = slice(8 * h, 8 * h + 8)
                            send2[at_part, at, half, :] = stow(
                                2 * at_part - 2 + h, send2[at_part, at, half, :], extra)
                        return carry

                    lax.fori_loop(0, 8, stow_back, 0)
                send_all(at_part, 16 if at_part > 0 else 8, send2, recv2, s_back)

        return carry

    lax.fori_loop(0, PARTS, one_part, 0)

    far_own.wait()
    wait_rows(far_recv, 7, 0, 6, s_far.at[1, 0])

    @pl.when(b >= 6)
    def _():
        wait_rows(far_recv, 1, 6, 1, s_far.at[1, 1])

    @pl.when(b < 6)
    def _():
        wait_rows(far_recv, 2, 6, 1, s_far.at[1, 1])

    for p in range(2):
        for c in range(2):
            for k in range(2):
                for g in range(8):
                    first, count = 6 * g + max(g - 6, 0), 6 + (g >= 6)
                    far[p, c, k, first:first + count, :] = far_recv[g, 0:count, k, c, p, :]

    loads[5].wait()
    acc[...] = jnp.zeros_like(acc)

    def narrow_tile(part, c):
        got = recv2[part, :, c * 8:c * 8 + 8, :].reshape(32, 2, 8, LANES)
        even, odd = got[:, 0], got[:, 1]
        m = lower[None]
        for k in range(2):
            rows = jnp.where(m, even, odd) if k == 0 else jnp.where(m, odd, even)
            high, low = split(rows.reshape(256, LANES))
            both = mul(narrow[k, part], high)
            acc[c, k] = acc[c, k] + (both[:T_CHILD] + both[T_CHILD:] + mul(narrow[k, part, 0:T_CHILD, :], low))

    wait_all(0, 8, recv2, s_back.at[1, 0])
    narrow_tile(0, 0)

    def hand_over(c):
        return pltpu.make_async_remote_copy(
            src_ref=own.at[1 - core, c], dst_ref=res_recv.at[c], send_sem=s_swap.at[2 + c], recv_sem=s_swap.at[4 + c],
            device_id=buddy, device_id_type=MESH)

    def finish(c):
        for k in range(2):
            full = jnp.transpose(acc[c, k])
            own[0, c, k, 0:50, :] = full[0:50]
            own[1, c, k, 0:50, :] = full[50:100]
        hand_over(c).start()

    def keep(c):
        for p in range(2):
            @pl.when(core == p)
            def _():
                for k in range(2):
                    out[:, k, c, p, :] = own[p, c, k, 0:50, :] + far[p, c, k, 0:50, :]

    def take_over(c):
        hand_over(c).wait()
        for p in range(2):
            @pl.when(core != p)
            def _():
                for k in range(2):
                    out[:, k, c, p, :] = res_recv[c, k, 0:50, :] + far[p, c, k, 0:50, :]

    wait_all(1, 16, recv2, s_back.at[1, 1])
    narrow_tile(1, 0)
    narrow_tile(1, 1)

    def take_back(part, i, carry):
        at = pl.ds(i * 8, 8)
        extra = jnp.zeros((8, 8, LANES), F32) if part == 1 else recv2[0, at, 8:16, :]
        for h in range(2):
            extra = unstow(2 * part - 2 + h, recv2[part, at, 8 * h:8 * h + 8, :], extra)
        recv2[0, at, 8:16, :] = extra
        return carry

    lax.fori_loop(0, 8, functools.partial(take_back, 1), 0)
    wait_all(2, 16, recv2, s_back.at[1, 2])
    narrow_tile(2, 0)
    finish(0)

    lax.fori_loop(0, 8, functools.partial(take_back, 2), 0)
    narrow_tile(2, 1)
    narrow_tile(0, 1)
    finish(1)
    keep(0)
    keep(1)
    take_over(0)
    take_over(1)

    for part in range(PARTS):
        wait_all(part, 8 if part == 2 else 16, send1, s_main.at[0, part])
        wait_all(part, 8 if part == 0 else 16, send2, s_back.at[0, part])
    wait_rows(child_recv, 7, 0, 6, s_child.at[0, 0])
    wait_rows(far_recv, 7, 0, 6, s_far.at[0, 0])

    @pl.when(b >= 6)
    def _():
        wait_rows(child_recv, 1, 6, 1, s_child.at[0, 1])
        wait_rows(far_recv, 7, 6, 1, s_far.at[0, 1])

    @pl.when(b < 6)
    def _():
        wait_rows(child_recv, 2, 6, 1, s_child.at[0, 1])

    span = tab_recv.at[core, pl.ds(0, 7)]
    pltpu.make_async_copy(span, span, s_tab.at[0]).wait()


def shards(child_rad, box_at_slot, octant, far_par, far_par_off, far_child, far_child_off, far_child_count,
           trans_par, trans_child):
    wide, narrow = theta_tables()
    vmem = pl.BlockSpec(memory_space=pltpu.VMEM)
    smem = pl.BlockSpec(memory_space=pltpu.SMEM)
    anywhere = pl.BlockSpec(memory_space=pl.ANY)
    chunks = pltpu.VMEM((PARTS, 64, 16, LANES), F32)
    groups = pltpu.VMEM((8, GROUP, 2, 2, 2, T_CHILD), F32)
    there, back = phi_tables()
    out = pl.pallas_call(
        kernel,
        out_shape=pltpu.VMEM((50, 2, 2, 2, T_CHILD), F32),
        in_specs=[smem] * 7 + [anywhere] * 7 + [vmem],
        out_specs=vmem,
        scratch_shapes=[
            pltpu.SMEM((8,), jnp.int32),
            pltpu.SMEM((8,), jnp.int32),
            pltpu.SMEM((8,), jnp.int32),
            pltpu.SMEM((24,), jnp.int32),
            pltpu.SMEM((24,), jnp.int32),
            pltpu.SMEM((112,), jnp.int32),
            pltpu.SMEM((112,), jnp.int32),
            pltpu.SMEM((112,), jnp.int32),
            pltpu.SMEM((112,), F32),
            pltpu.VMEM((50, 2, 2, 2, T_CHILD), F32),
            pltpu.VMEM((100, 8, 2, 256), F32),
            pltpu.VMEM((GROUP, 16, 2, T_CHILD), F32),
            pltpu.VMEM(wide.shape, BF16),
            pltpu.VMEM(narrow.shape, BF16),
            pltpu.VMEM(there.shape, BF16),
            pltpu.VMEM(back.shape, BF16),
            pltpu.VMEM((2, 2, 2, 56, T_CHILD), F32),
            pltpu.VMEM((2, 2, 56, T_CHILD), F32),
            pltpu.VMEM((2, 2, T_CHILD, LANES), BF16),
            pltpu.VMEM((2, 2, T_CHILD, LANES), BF16),
            chunks, chunks, chunks, chunks,
            groups,
            pltpu.VMEM((8, 2, 2, 2, 8, T_CHILD), F32),
            pltpu.VMEM((16, 2, 8, T_CHILD), F32),
            groups,
            groups,
            pltpu.VMEM((2, 2, 2, 56, T_CHILD), F32),
            pltpu.VMEM((2, LANES, 256), F32),
            pltpu.VMEM((2, 4, 8, PARTS, 8, LANES), F32),
            pltpu.VMEM((2, 8, 8, PARTS, 8, LANES), F32),
            pltpu.VMEM((8, 2, 8, 16 * LANES), F32),
            pltpu.VMEM((PARTS, 8, 2, 8, 16 * LANES), F32),
            pltpu.VMEM((2, 128, 8 * LANES), F32),
            pltpu.VMEM((2, 8, 2, 8, LANES), F32),
            pltpu.VMEM((2, 256, 8 * LANES), BF16),
            pltpu.VMEM((2, 2, T_CHILD, LANES), F32),
            pltpu.VMEM((2, 2, 2, 56, T_CHILD), F32),
            pltpu.VMEM((2, 2, 56, T_CHILD), F32),
            pltpu.SemaphoreType.DMA((7,)),
            pltpu.SemaphoreType.DMA((6,)),
            pltpu.SemaphoreType.DMA((2, 2)),
            pltpu.SemaphoreType.DMA((2, 2)),
            pltpu.SemaphoreType.DMA((2,)),
            pltpu.SemaphoreType.DMA((2,)),
            pltpu.SemaphoreType.DMA((2, PARTS)),
            pltpu.SemaphoreType.DMA((2, PARTS)),
            pltpu.SemaphoreType.DMA((2,)),
        ],
        compiler_params=pltpu.CompilerParams(
            collective_id=0, has_side_effects=True, vmem_limit_bytes=60 * 2**20),
        cost_estimate=pl.CostEstimate(flops=14_000_000_000, bytes_accessed=16_000_000, transcendentals=0),
        name="fields",
    )(box_at_slot, octant, far_par.T, far_par_off.T, far_child.T, far_child_off.T, far_child_count,
      child_rad, trans_par, trans_child,
      jnp.asarray(wide), jnp.asarray(narrow), jnp.asarray(there), jnp.asarray(back), jnp.asarray(phi_angles()))
    return out


def solution(mesh):
    return jax.shard_map(
        shards,
        mesh=mesh,
        in_specs=(P("dir", "box", None, None, None), P(), P(), P(), P(), P(), P(), P(),
                  P("dir", None, None, None), P("dir", None, None, None)),
        out_specs=P("dir", "box", None, None, None),
        check_vma=False,
    )
```
